256 devices in a mesh: region: 8 (over z), plant: 32 (over x, y, core).
Axes of the slice: x: 4, y: 4, z: 8, core: 2. Of those that a mesh axis runs over, the one named last changes fastest.
Arguments:
- dispatch_start: float32 [16384, 288], P(('region', 'plant')), may hold values from 0 to 1
- marginal_cost: float32 [16384], P(('region', 'plant')), may hold values from 0.3 to 3
- quad_cost: float32 [16384], P(('region', 'plant')), may hold values from 0.5 to 2
- capacity: float32 [16384], P(('region', 'plant')), may hold values from 0.5 to 4
- band_widths: int32 [16384], P(('region', 'plant')), may hold values from 1 to 12
- ramp_band: float32 [25, 288], replicated, may hold values from -0.12 to 0.12
- plant_bus: int32 [16384], P(('region', 'plant')), may hold values from 0 to 2047
- plant_counts: int32 [256], P(('region', 'plant')), may hold values from 8 to 64, as said below
- load: float32 [16384, 288], P('region'), may hold values from -6 to 6
- ptdf: bfloat16 [16384, 16384], P('plant', 'region'), may hold values from -0.046875 to 0.046875
- line_limit: float32 [16384, 288], P('plant'), may hold values from 0.5 to 4
- line_price_start: float32 [16384, 288], P('plant'), may hold values from -3 to 3
- bus_price_start: float32 [16384, 288], P(('region', 'plant')), may hold values from 0 to 2
- energy_price: float32 [288], replicated, may hold values from 0.5 to 3
Outputs:
- dispatch: float32 [16384, 288], P(('region', 'plant'))
- line_price: float32 [16384, 288], P('plant')
- bus_price: float32 [16384, 288], P(('region', 'plant'))
The draws below stay inside these ranges and needn't reach their ends.
Inputs may be any that keep to these rules, and one draw needn't show every extreme that they name: `plant_counts`: number of live plants in each block of 64 plant slots, live slots first; some block is full in every draw. `plant_bus`: bus of plant i among the 2048 buses of region i // 2048.
All inputs are finite; a program needn't handle non-finite values.
Results may differ from the reference program's by a relative error of at most 0.0037.
Values may be sent and summed in bfloat16 or wider, within the bound.
A program may use at most 64 MiB of HBM per device.

```python
import math
import jax
import jax.numpy as jnp
from jax import lax

H = 288
WMAX = 12
ITERS = 3
OUTER = 2
PLANT_DEV = 64
BUS_DEV = 2048
PLANTS = 16384
BUSES = 16384
LINES = 16384
N_REGION = 8
N_PLANT = 32


def draw_plant_counts(key, part):
    key = jax.random.fold_in(key, 7)
    total_blocks = N_REGION * N_PLANT
    lowest = max(PLANT_DEV // 8, 1)
    first_key, second_key, third_key = jax.random.split(key, 3)
    spread = PLANT_DEV - lowest + 1
    draw_one = jax.random.randint(first_key, (total_blocks,), 0, spread)
    draw_two = jax.random.randint(second_key, (total_blocks,), 0, spread)
    counts = lowest + jnp.minimum(draw_one, draw_two)
    chosen = jax.random.randint(third_key, (), 0, total_blocks)
    return counts.at[chosen].set(PLANT_DEV).astype(jnp.int32)


def touch_ends(array, rng, low, top_value):
    dims = array.shape
    index_at = [jax.random.randint(jax.random.fold_in(rng, axis), (), 0, dims[axis]) for axis in range(len(dims))]
    array = array.at[tuple(index_at)].set(low)
    longest = dims.index(max(dims))
    index_at[longest] = (index_at[longest] + 1) % dims[longest]
    return array.at[tuple(index_at)].set(top_value)


def level_of(rng, dims, shards, low, high):
    factor_of = 1.0
    for dim, shards_of in shards:
        steps = jax.random.uniform(jax.random.fold_in(jax.random.fold_in(rng, 6), dim), (shards_of,), jnp.float32, low / len(shards), high / len(shards))
        factor_of = factor_of * jnp.repeat(jnp.exp(steps), dims[dim] // shards_of).reshape((-1,) + (1,) * (len(dims) - 1 - dim))
    return factor_of


def bell_draw(own_key, shape, scale, most, cuts=(), kind=jnp.bfloat16):
    entries = scale * jax.random.normal(own_key, shape, jnp.float32)
    if cuts:
        entries = entries * level_of(own_key, shape, cuts, -0.22, 0.18)
    return jnp.clip(entries, -most, most).astype(kind)


def setup_inputs(seed: int = 0) -> dict:
    arg_keys = jax.random.split(jax.random.key(seed), 15)
    dispatch_start = jnp.clip(1.0 * jax.random.uniform(arg_keys[0], (PLANTS, H), jnp.float32) ** level_of(arg_keys[0], (PLANTS, H), ((0, 256),), -0.2, 0.2), 0.0, 1.0)
    marginal_cost = jnp.clip(jnp.exp(math.log(3.0) - 2.3025851 * jax.random.uniform(arg_keys[1], (PLANTS,), jnp.float32) ** level_of(arg_keys[1], (PLANTS,), ((0, 256),), -0.2, 0.2)), 0.3, 3.0)
    quad_cost = jnp.clip(jnp.exp(math.log(2.0) - 1.3862944 * jax.random.uniform(arg_keys[2], (PLANTS,), jnp.float32) ** level_of(arg_keys[2], (PLANTS,), ((0, 256),), -0.2, 0.2)), 0.5, 2.0)
    capacity = jnp.clip(jnp.exp(math.log(4.0) - 2.0794415 * jax.random.uniform(arg_keys[3], (PLANTS,), jnp.float32) ** level_of(arg_keys[3], (PLANTS,), ((0, 256),), -0.2, 0.2)), 0.5, 4.0)
    band_widths = touch_ends(jax.random.randint(arg_keys[4], (PLANTS,), 1, WMAX + 1), jax.random.fold_in(arg_keys[4], 1), 1, WMAX).astype(jnp.int32)
    ramp_band = jnp.clip(jax.random.uniform(arg_keys[5], (2 * WMAX + 1, H), jnp.float32, -0.12, 0.12), -0.12, 0.12)
    plant_bus = touch_ends(jax.random.randint(arg_keys[6], (PLANTS,), 0, BUS_DEV), jax.random.fold_in(arg_keys[6], 1), 0, BUS_DEV - 1).astype(jnp.int32)
    plant_counts = draw_plant_counts(jax.random.fold_in(arg_keys[14], 71), 0)
    load = bell_draw(arg_keys[8], (BUSES, H), 1.0, 6.0, ((0, 8),), jnp.float32)
    ptdf = bell_draw(arg_keys[9], (LINES, BUSES), LINES ** -0.5, 0.046875, ((0, 32), (1, 8)))
    line_limit = jnp.clip(jnp.exp(math.log(4.0) - 2.0794415 * jax.random.uniform(arg_keys[10], (LINES, H), jnp.float32) ** level_of(arg_keys[10], (LINES, H), ((0, 32),), -0.2, 0.2)), 0.5, 4.0)
    line_price_start = bell_draw(arg_keys[11], (LINES, H), 0.5, 3.0, ((0, 32),), jnp.float32)
    bus_price_start = jnp.clip(2.0 * jax.random.uniform(arg_keys[12], (BUSES, H), jnp.float32) ** level_of(arg_keys[12], (BUSES, H), ((0, 256),), -0.2, 0.2), 0.0, 2.0)
    energy_price = jnp.clip(jnp.exp(jax.random.uniform(arg_keys[13], (H,), jnp.float32, math.log(0.5), math.log(3.0))), 0.5, 3.0)
    return dict(dispatch_start=dispatch_start, marginal_cost=marginal_cost, quad_cost=quad_cost, capacity=capacity, band_widths=band_widths, ramp_band=ramp_band, plant_bus=plant_bus, plant_counts=plant_counts, load=load, ptdf=ptdf, line_limit=line_limit, line_price_start=line_price_start, bus_price_start=bus_price_start, energy_price=energy_price)


STEP_SIZE = 0.5


def ramp_band_apply(values, band_table, widths):
    reach = (band_table.shape[0] - 1) // 2
    length = values.shape[1]
    padded = jnp.pad(values, ((0, 0), (reach, reach)))
    result = (1.0 + band_table[reach])[None, :] * values
    for offset in range(1, reach + 1):
        keep = (widths >= offset).astype(jnp.float32)[:, None]
        later = padded[:, reach + offset: reach + offset + length]
        earlier = padded[:, reach - offset: reach - offset + length]
        result = result + keep * (band_table[reach + offset][None, :] * later + band_table[reach - offset][None, :] * earlier)
    return result


def plant_sweeps(dispatch, plant_price, marginal_cost, quad_cost, capacity, band_table, widths, live):
    for sweep in range(ITERS):
        moved = dispatch + STEP_SIZE * (plant_price - marginal_cost[:, None] - quad_cost[:, None] * dispatch)
        dispatch = live * jnp.clip(ramp_band_apply(moved, band_table, widths), 0.0, capacity[:, None])
    return dispatch


def soft_limit(line_price, flow, line_limit):
    shifted = line_price + flow
    return shifted - jnp.clip(shifted, -line_limit, line_limit)


def reference(dispatch_start, marginal_cost, quad_cost, capacity, band_widths, ramp_band, plant_bus, plant_counts, load, ptdf, line_limit, line_price_start, bus_price_start, energy_price):
    plant_total = dispatch_start.shape[0]
    slot = jnp.arange(plant_total, dtype=jnp.int32)
    live = ((slot % PLANT_DEV) < plant_counts[slot // PLANT_DEV]).astype(jnp.float32)[:, None]
    bus_of = ((slot // (PLANT_DEV * N_PLANT)) * BUS_DEV + plant_bus).astype(jnp.int32)
    dispatch = dispatch_start
    line_price = line_price_start
    bus_price = bus_price_start
    for outer in range(OUTER):
        plant_price = bus_price[bus_of]
        dispatch = plant_sweeps(dispatch, plant_price, marginal_cost, quad_cost, capacity, ramp_band, band_widths, live)
        summed = jax.ops.segment_sum(dispatch, bus_of, num_segments=BUSES)
        injection = (summed - load).astype(jnp.bfloat16)
        flow = jnp.dot(ptdf, injection, preferred_element_type=jnp.float32)
        line_price = soft_limit(line_price, flow, line_limit)
        sent_price = line_price.astype(jnp.bfloat16)
        congestion = lax.dot_general(ptdf, sent_price, (((0,), (0,)), ((), ())), preferred_element_type=jnp.float32)
        bus_price = energy_price[None, :] - congestion
    return dispatch, line_price, bus_price
```

```python
import jax
import jax.numpy as jnp
from jax import lax
from jax.experimental import pallas as pl
from jax.experimental.pallas import tpu as pltpu
from jax.sharding import PartitionSpec as P

H = 288
HALF = 144
EXT = 192
REACH = 12
ITERS = 3
ROWS_A = 80
F32 = jnp.float32
BF16 = jnp.bfloat16
HALVES = ((0, ROWS_A), (ROWS_A, HALF - ROWS_A))
HALVES_EXT = ((0, 96), (96, 96))
NN = (((1,), (0,)), ((), ()))
NT = (((1,), (1,)), ((), ()))


def body(
    dispatch_in, bus_price_in, params_in, ramp_in, energy_in, load_in, ptdf_in, limit_in, lp_in,
    dispatch_out, line_out, bus_out,
    stage, xd, xp, rxd, rxp, pmo, rpm, pm, ids, ramp_t, kt, vb, dsp, px, oh,
    pt, q, ld, lim, lps, slim, slps, f0,
    ga, gb0, gb1, fb, rc0, rc1, sa0, sa1, pb, r1a, r1b, t2a, t2b, r2a, r2b,
    halo_s, halo_p, halo_d, fin_s, fin_r, fd_s, fd_r, lr,
    loc, ex_s, ex_r, id_s, id_r, ag_s, ag_r, zs_s, zs_r, rs_s, rs_r,
):
    z = lax.axis_index("region")
    p = lax.axis_index("plant")
    x = p // 8
    y = (p // 2) % 4
    c = p % 2
    other = 1 - c

    def dev(zz, xx, yy, cc):
        return (zz, (xx * 4 + yy) * 2 + cc)

    sibling = dev(z, x, y, other)

    def xn(d):
        return (x + d) % 4

    def yn(d):
        return (y + d) % 4

    def remote(src, dst, send, recv, device):
        return pltpu.make_async_remote_copy(
            src_ref=src, dst_ref=dst, send_sem=send, recv_sem=recv,
            device_id=device, device_id_type=pl.DeviceIdType.MESH,
        )

    sends = []

    def push(src, dst, send, recv, device):
        copy = remote(src, dst, send, recv, device)
        copy.start()
        sends.append(copy)
        return copy

    def drain():
        for copy in sends:
            copy.wait_send()
        sends.clear()

    def arrived(dst, recv):
        remote(dst, dst, ex_s.at[0], recv, sibling).wait_recv()

    own_row = pl.multiple_of(HALF * c, 16)
    other_row = pl.multiple_of(HALF * other, 16)
    line_lane = pl.multiple_of(128 * (z % 4), 128)
    own_block = pl.ds(pl.multiple_of(512 * c, 512), 512)
    local = [
        pltpu.make_async_copy(ptdf_in, pt.at[own_block], loc.at[0]),
        pltpu.make_async_copy(load_in.at[pl.ds(own_row, HALF)], ld, loc.at[1]),
        pltpu.make_async_copy(
            limit_in.at[pl.ds(own_row, HALF), pl.ds(line_lane, 128)], lim, loc.at[2]),
        pltpu.make_async_copy(
            lp_in.at[pl.ds(own_row, HALF), pl.ds(line_lane, 128)], lps, loc.at[3]),
    ]
    for copy in local:
        copy.start()

    barrier = pltpu.get_barrier_semaphore()
    peers = [sibling]
    peers += [dev(z, xn(d), y, c) for d in (1, 2, 3)]
    peers += [dev(z, x, yn(d), c) for d in (1, 2, 3)]
    peers += [dev((z + d) % 8, x, y, c) for d in range(1, 8)]
    for peer in peers:
        pl.semaphore_signal(barrier, inc=1, device_id=peer, device_id_type=pl.DeviceIdType.MESH)

    own_lanes = pl.ds(pl.multiple_of(64 * c, 64), 64)
    own_ext = pl.ds(pl.multiple_of(96 * c, 96), EXT)
    other_ext = pl.ds(pl.multiple_of(96 * other, 96), EXT)
    stage[...] = jnp.zeros_like(stage)
    stage[own_lanes, 0:H] = bus_price_in[...]
    xp[...] = stage[...].T
    rows = params_in[...]
    gap = jnp.zeros_like(rows)
    pmo[...] = jnp.where(
        c == 0, jnp.concatenate([rows, gap], axis=1), jnp.concatenate([gap, rows], axis=1))
    pl.semaphore_wait(barrier, len(peers))
    push(xp.at[other_ext], rxp, ex_s.at[0], ex_r.at[0], sibling)
    push(pmo, rpm, ex_s.at[1], ex_r.at[1], sibling)
    stage[own_lanes, 0:H] = dispatch_in[...]
    xd[...] = stage[...].T
    push(xd.at[other_ext], rxd, ex_s.at[2], ex_r.at[2], sibling)
    push(ptdf_in, pt.at[own_block], ex_s.at[3], ex_r.at[3], sibling)
    push(limit_in.at[pl.ds(other_row, HALF), pl.ds(line_lane, 128)], slim, ex_s.at[4], ex_r.at[4], sibling)
    push(lp_in.at[pl.ds(other_row, HALF), pl.ds(line_lane, 128)], slps, ex_s.at[5], ex_r.at[5], sibling)

    def gather_start(grid, halves, k):
        for part in (0, 1):
            for h, (row, count) in enumerate(halves):
                block = grid.at[x, y, pl.ds(row, count)]
                for i, d in enumerate((2, 1, 3)):
                    along_x = h == part
                    device = dev(z, xn(d), y, c) if along_x else dev(z, x, yn(d), c)
                    push(block, block, ag_s.at[k, 6 * part + 3 * h + i], ag_r.at[k, h, x, y], device)

    def gather_forward(grid, halves, k):
        n = 12
        for d in (1, 3, 2):
            for h, (row, count) in enumerate(halves):
                sx, sy = (xn(d), y) if h == 0 else (x, yn(d))
                block = grid.at[sx, sy, pl.ds(row, count)]
                arrived(block, ag_r.at[k, h, sx, sy])
                for e in (2, 1, 3):
                    device = dev(z, x, yn(e), c) if h == 0 else dev(z, xn(e), y, c)
                    push(block, block, ag_s.at[k, n], ag_r.at[k, h, sx, sy], device)
                    n += 1

    def gather_finish(grid, halves, k):
        for h, (row, count) in enumerate(halves):
            for d in (1, 3, 2):
                sx, sy = (x, yn(d)) if h == 0 else (xn(d), y)
                arrived(grid.at[sx, sy, pl.ds(row, count)], ag_r.at[k, h, sx, sy])
            for d in (1, 3, 2):
                for e in (1, 3, 2):
                    arrived(grid.at[xn(d), yn(e), pl.ds(row, count)], ag_r.at[k, h, xn(d), yn(e)])

    def wide(ref, rows=None):
        if len(ref.shape) == 4:
            return jnp.concatenate([ref[i, j] for i in range(4) for j in range(4)], axis=1)
        return jnp.concatenate([ref[i] for i in range(8)], axis=1)

    arrived(rxp, ex_r.at[0])
    ga[x, y] = (xp[own_ext] + rxp[...]).astype(BF16)
    gather_start(ga, HALVES_EXT, 0)
    arrived(rpm, ex_r.at[1])
    pm[...] = pmo[...] + rpm[...]
    ids[x, y] = pm[...]
    for i, d in enumerate((2, 1, 3)):
        push(ids.at[x, y], ids.at[x, y], id_s.at[i], id_r.at[i], dev(z, xn(d), y, c))

    stage[...] = jnp.zeros_like(stage)
    stage[0:25, 0:H] = ramp_in[...]
    stage[32:33, 0:H] = energy_in[...]
    ramp_t[...] = stage[...].T
    marginal, quad, cap, width, live = (pm[i:i + 1] for i in range(5))
    for d in range(0, REACH + 1):
        keep = (width > d - 0.5).astype(F32)
        for s in ((0,) if d == 0 else (d, -d)):
            row = REACH + s
            column = ramp_t[own_ext, row:row + 1]
            if d == 0:
                kt[row] = jnp.broadcast_to(1.0 + column, (EXT, 128))
            else:
                kt[row] = column * keep
    energy = ramp_t[pl.ds(own_row, HALF), 32:33]

    gather_forward(ga, HALVES_EXT, 0)
    for i, d in enumerate((2, 1, 3)):
        arrived(ids.at[xn(4 - d), y], id_r.at[i])
    for i, d in enumerate((2, 1, 3)):
        push(ids.at[:, y], ids.at[:, y], id_s.at[3 + i], id_r.at[3 + i], dev(z, x, yn(d), c))
    bus_row = lax.broadcasted_iota(jnp.int32, (2048, 128), 0)
    oh[...] = jnp.where(bus_row == pm[5:6].astype(jnp.int32), 1.0, 0.0).astype(BF16)

    for copy in local:
        copy.wait()
    load_half = ld[...].astype(BF16)
    arrived(pt.at[pl.ds(pl.multiple_of(512 * other, 512), 512)], ex_r.at[3])

    def load_flow(i, _):
        block = pt[pl.ds(pl.multiple_of(256 * i, 256), 256)]
        f0[i] = lax.dot_general(load_half, block, NT, preferred_element_type=F32)
        return 0

    lax.fori_loop(0, 4, load_flow, 0)

    for i, d in enumerate((2, 1, 3)):
        arrived(ids.at[:, yn(4 - d)], id_r.at[3 + i])

    def plant_columns(i, _):
        bus = jnp.concatenate(
            [ids[i // 2, 2 * (i % 2), 5:6], ids[i // 2, 2 * (i % 2) + 1, 5:6]], axis=1)
        iota = lax.broadcasted_iota(jnp.int32, (2048, 256), 0)
        one_hot = jnp.where(iota == bus.astype(jnp.int32), 1.0, 0.0).astype(BF16)
        q[:, pl.ds(pl.multiple_of(256 * i, 256), 256)] = jnp.dot(
            pt[...], one_hot, preferred_element_type=F32).astype(BF16)
        return 0

    lax.fori_loop(0, 4, plant_columns, 0)

    arrived(rxd, ex_r.at[2])
    dsp[...] = xd[own_ext] + rxd[...]
    arrived(slim, ex_r.at[4])
    arrived(slps, ex_r.at[5])
    holds = c == z // 4
    limit = jnp.where(holds, lim[...], slim[...])
    line_price = jnp.where(holds, lps[...], slps[...])
    lim[...] = limit
    lps[...] = line_price

    gather_finish(ga, HALVES_EXT, 0)
    drain()
    px[...] = jnp.dot(wide(ga), oh[...], preferred_element_type=F32)
    vb[...] = jnp.zeros_like(vb)

    core_row = pl.multiple_of(48 * c, 16)
    halo_row = pl.multiple_of(48 + 48 * other, 16)
    halo_at = pl.multiple_of(HALF * other, 16)

    def sweep(_, carry):
        d = dsp[...]
        vb[16:16 + EXT] = d + 0.5 * (px[...] - marginal - quad * d)
        for r in range(0, EXT, 64):
            total = kt[REACH, r:r + 64] * vb[16 + r:16 + r + 64]
            for s in range(1, REACH + 1):
                for o in (s, -s):
                    total = total + kt[REACH + o, r:r + 64] * vb[16 + o + r:16 + o + r + 64]
            dsp[r:r + 64] = live * jnp.clip(total, 0.0, cap)
        return carry

    def limit_lines(k, price, grid, sent, received):
        spread = wide(grid)
        for dq in (2, 1, 3, 0):
            pair = (z // 2 + dq) % 4
            block = q[pl.ds(pl.multiple_of(256 * pair, 256), 256)]
            part = lax.dot_general(spread, block, NT, preferred_element_type=F32) - f0[pair]
            for j in (0, 1):
                fb[k, 2 * pair + j] = part[:, 128 * j:128 * j + 128].astype(BF16)
            for j in (0, 1):
                target = 2 * pair + j
                away = (target - z + 8) % 8

                @pl.when(away != 0)
                def _():
                    remote(fb.at[k, target], received.at[z], zs_s.at[k, 0, target], zs_r.at[k, 0, z],
                           dev(target, x, y, c)).start()

        flow = fb[k, z].astype(F32)
        for d in (1, 7, 2, 6, 3, 5, 4):
            source = (z + d) % 8
            arrived(received.at[source], zs_r.at[k, 0, source])
            flow = flow + received[source].astype(F32)
        shifted = price + flow
        new = shifted - jnp.clip(shifted, -lim[...], lim[...])
        sent[z] = new.astype(BF16)
        for d in (4, 3, 5, 2, 6, 1, 7):
            target = (z + d) % 8
            push(sent.at[z], sent.at[z], zs_s.at[k, 1, target], zs_r.at[k, 1, z], dev(target, x, y, c))
        for d in (1, 7, 2, 6, 3, 5, 4):
            source = (z + d) % 8
            arrived(sent.at[source], zs_r.at[k, 1, source])
        for d in range(1, 8):
            target = (z + d) % 8
            remote(fb.at[k, target], received.at[z], zs_s.at[k, 0, target], zs_r.at[k, 0, z],
                   dev(target, x, y, c)).wait_send()
        drain()
        return new

    def congestion(k, sent, matrix):
        spread = wide(sent)
        for d in (2, 1, 3, 0):
            gx = xn(d)
            for h in (0, 1):
                columns = pl.ds(pl.multiple_of(512 * gx + 256 * h, 256), 256)
                part = jnp.dot(spread, matrix[:, columns], preferred_element_type=F32).astype(BF16)
                pb[k, gx, 2 * h] = part[:, 0:128]
                pb[k, gx, 2 * h + 1] = part[:, 128:256]
            if d:
                push(pb.at[k, gx, :, pl.ds(0, ROWS_A)], r1a.at[k, d - 1], rs_s.at[k, 0, d - 1],
                     rs_r.at[k, 0, d - 1], dev(z, gx, y, c))
        for d in (2, 1, 3):
            push(pb.at[k, :, yn(d), pl.ds(ROWS_A, HALF - ROWS_A)], r1b.at[k, d - 1], rs_s.at[k, 1, d - 1],
                 rs_r.at[k, 1, d - 1], dev(z, x, yn(d), c))
        for d in (1, 3, 2):
            arrived(r1a.at[k, d - 1], rs_r.at[k, 0, d - 1])
        tops = {}
        for e in (2, 1, 3, 0):
            total = pb[k, x, yn(e), 0:ROWS_A].astype(F32)
            for d in (1, 2, 3):
                total = total + r1a[k, d - 1, yn(e)].astype(F32)
            if e:
                t2a[k, e - 1] = total.astype(BF16)
                push(t2a.at[k, e - 1], r2a.at[k, e - 1], rs_s.at[k, 2, e - 1], rs_r.at[k, 2, e - 1],
                     dev(z, x, yn(e), c))
        top = total
        for d in (1, 3, 2):
            arrived(r1b.at[k, d - 1], rs_r.at[k, 1, d - 1])
        for e in (2, 1, 3, 0):
            total = pb[k, xn(e), y, ROWS_A:HALF].astype(F32)
            for d in (1, 2, 3):
                total = total + r1b[k, d - 1, xn(e)].astype(F32)
            if e:
                t2b[k, e - 1] = total.astype(BF16)
                push(t2b.at[k, e - 1], r2b.at[k, e - 1], rs_s.at[k, 3, e - 1], rs_r.at[k, 3, e - 1],
                     dev(z, xn(e), y, c))
        low = total
        for d in (1, 3, 2):
            arrived(r2a.at[k, d - 1], rs_r.at[k, 2, d - 1])
            top = top + r2a[k, d - 1].astype(F32)
        for d in (1, 3, 2):
            arrived(r2b.at[k, d - 1], rs_r.at[k, 3, d - 1])
            low = low + r2b[k, d - 1].astype(F32)
        return jnp.concatenate([top, low], axis=0)

    lax.fori_loop(0, ITERS, sweep, 0)
    gb0[x, y] = dsp[pl.ds(core_row, HALF)].astype(BF16)
    gather_start(gb0, HALVES, 1)
    halo_s[1] = dsp[pl.ds(halo_row, 48)]
    push(halo_s.at[1], halo_d, ex_s.at[6], ex_r.at[6], sibling)
    gather_forward(gb0, HALVES, 1)
    lax.fori_loop(4, 8, plant_columns, 0)
    gather_finish(gb0, HALVES, 1)
    lps[...] = limit_lines(0, lps[...], gb0, sa0, rc0)
    price = energy - congestion(0, sa0, q)
    px[pl.ds(core_row, HALF)] = price
    halo_s[0] = px[pl.ds(halo_row, 48)]
    push(halo_s.at[0], halo_p, ex_s.at[7], ex_r.at[7], sibling)
    arrived(halo_d, ex_r.at[6])
    dsp[pl.ds(halo_at, 48)] = halo_d[...]
    arrived(halo_p, ex_r.at[7])
    px[pl.ds(halo_at, 48)] = halo_p[...]

    lax.fori_loop(0, ITERS, sweep, 0)
    own = dsp[pl.ds(core_row, HALF)]
    gb1[x, y] = own.astype(BF16)
    gather_start(gb1, HALVES, 2)
    fd_s[...] = own
    push(fd_s, fd_r, ex_s.at[8], ex_r.at[8], sibling)
    gather_forward(gb1, HALVES, 2)

    def rows_out(mine, theirs):
        gap = jnp.zeros((96, 128), F32)
        first = jnp.where(c == 0, mine, theirs)
        second = jnp.where(c == 0, theirs, mine)
        return jnp.concatenate([first, second, gap], axis=0).T

    arrived(fd_r, ex_r.at[8])
    stage[...] = rows_out(fd_s[...], fd_r[...])
    dispatch_out[...] = stage[own_lanes, 0:H]
    gather_finish(gb1, HALVES, 2)
    limit_lines(1, lps[...], gb1, sa1, rc1)
    other_lines = pl.ds(pl.multiple_of(4 * other, 4), 4)
    push(sa1.at[other_lines], lr, ex_s.at[9], ex_r.at[9], sibling)
    cong = congestion(1, sa1, pt)
    fin_s[...] = energy - cong
    push(fin_s, fin_r, ex_s.at[10], ex_r.at[10], sibling)
    arrived(lr, ex_r.at[9])
    for i in range(4):
        lanes = slice(128 * i, 128 * i + 128)
        line_out[pl.ds(own_row, HALF), lanes] = sa1[4 * c + i].astype(F32)
        line_out[pl.ds(other_row, HALF), lanes] = lr[i].astype(F32)
    arrived(fin_r, ex_r.at[10])
    stage[...] = rows_out(fin_s[...], fin_r[...])
    bus_out[...] = stage[own_lanes, 0:H]
    drain()


def shards(
    dispatch_start, marginal_cost, quad_cost, capacity, band_widths, ramp_band, plant_bus, plant_counts,
    load, ptdf, line_limit, line_price_start, bus_price_start, energy_price,
):
    live = (jnp.arange(64, dtype=jnp.int32) < plant_counts[0]).astype(F32)
    nothing = jnp.zeros((64,), F32)
    params = jnp.stack([
        marginal_cost, quad_cost, capacity, band_widths.astype(F32), live, plant_bus.astype(F32),
        nothing, nothing,
    ])
    vmem = pl.BlockSpec(memory_space=pltpu.VMEM)
    hbm = pl.BlockSpec(memory_space=pl.ANY)
    sem = pltpu.SemaphoreType.DMA

    def v(shape, kind=F32):
        return pltpu.VMEM(shape, kind)

    low = HALF - ROWS_A
    scratch = [
        v((128, 384)), v((384, 128)), v((384, 128)), v((EXT, 128)), v((EXT, 128)),
        v((8, 128)), v((8, 128)), v((8, 128)), v((4, 4, 8, 128)),
        v((384, 128)), v((25, EXT, 128)), v((EXT + 32, 128)), v((EXT, 128)), v((EXT, 128)),
        v((2048, 128), BF16),
        v((1024, 2048), BF16), v((1024, 2048), BF16), v((HALF, 2048)),
        v((HALF, 128)), v((HALF, 128)), v((HALF, 128)), v((HALF, 128)), v((4, HALF, 256)),
        v((4, 4, EXT, 128), BF16), v((4, 4, HALF, 128), BF16), v((4, 4, HALF, 128), BF16),
        v((2, 8, HALF, 128), BF16), v((8, HALF, 128), BF16), v((8, HALF, 128), BF16),
        v((8, HALF, 128), BF16), v((8, HALF, 128), BF16),
        v((2, 4, 4, HALF, 128), BF16),
        v((2, 3, 4, ROWS_A, 128), BF16), v((2, 3, 4, low, 128), BF16),
        v((2, 3, ROWS_A, 128), BF16), v((2, 3, low, 128), BF16),
        v((2, 3, ROWS_A, 128), BF16), v((2, 3, low, 128), BF16),
        v((2, 48, 128)), v((48, 128)), v((48, 128)),
        v((HALF, 128)), v((HALF, 128)), v((HALF, 128)), v((HALF, 128)),
        v((4, HALF, 128), BF16),
        sem((4,)), sem((11,)), sem((11,)), sem((6,)), sem((6,)), sem((3, 30)), sem((3, 2, 4, 4)),
        sem((2, 2, 8)), sem((2, 2, 8)), sem((2, 4, 3)), sem((2, 4, 3)),
    ]
    dispatch, line_price, bus_price = pl.pallas_call(
        body,
        out_shape=(
            jax.ShapeDtypeStruct((64, H), F32),
            jax.ShapeDtypeStruct((H, 512), F32),
            jax.ShapeDtypeStruct((64, H), F32),
        ),
        in_specs=[vmem] * 5 + [hbm] * 4,
        out_specs=(vmem,) * 3,
        scratch_shapes=scratch,
        compiler_params=pltpu.CompilerParams(
            collective_id=0, has_side_effects=True, vmem_limit_bytes=50 * 2**20),
        name="dispatch_window",
    )(
        dispatch_start, bus_price_start, params, ramp_band, energy_price[None], load.T, ptdf,
        line_limit.T, line_price_start.T,
    )
    return dispatch, line_price.T, bus_price


def solution(mesh):
    placed = (
        P(("region", "plant"), None),
        P(("region", "plant")),
        P(("region", "plant")),
        P(("region", "plant")),
        P(("region", "plant")),
        P(),
        P(("region", "plant")),
        P(("region", "plant")),
        P("region", None),
        P("plant", "region"),
        P("plant", None),
        P("plant", None),
        P(("region", "plant"), None),
        P(),
    )
    return jax.shard_map(
        shards,
        mesh=mesh,
        in_specs=placed,
        out_specs=(P(("region", "plant"), None), P("plant", None), P(("region", "plant"), None)),
        check_vma=False,
    )
```

```python
import jax
import jax.numpy as jnp
from jax import lax
from jax.experimental import pallas as pl
from jax.experimental.pallas import tpu as pltpu
from jax.sharding import PartitionSpec as P

H = 288
HALF = 144
EXT = 192
PARTS = 3
PART = 48
REACH = 12
ITERS = 3
F32 = jnp.float32
BF16 = jnp.bfloat16
NN = (((1,), (0,)), ((), ()))
NT = (((1,), (1,)), ((), ()))
FAR_FIRST = (2, 1, 3)


def body(
    dispatch_in, bus_price_in, marginal_in, quad_in, cap_in, width_in, bus_in, count_in, ramp_in,
    load_in, ptdf_in, limit_in, lp_in,
    dispatch_out, line_out, bus_out,
    dstage, pstage, prow, irow, crow, ramp_v, stage, xd, xp, rxd, rxp, pmo, rpm, pm, ids, ramp_t, kt, vb, dsp, px, oh,
    pt, q, qt, ld, lim, lps, slim, slps, f0, f0full,
    ga, gb, fb, rc, sa, pb, rp,
    halo_s, halo_p, halo_d, fin_s, fin_r, fd_s, fd_r, lr,
    loc, ex_s, ex_r, id_s, id_r, q_s, q_r, ag_s, ag_r, zr_s, zr_r, zg_s, zg_r, rs_s, rs_r,
):
    z = lax.axis_index("region")
    p = lax.axis_index("plant")
    g = p // 2
    x = g // 4
    y = g % 4
    c = p % 2
    other = 1 - c

    def dev(zz, gg, cc):
        return (zz, gg * 2 + cc)

    sibling = dev(z, g, other)

    def chip(dx, dy):
        return ((x + dx) % 4) * 4 + (y + dy) % 4

    others = [(dx, dy) for dx in (2, 1, 3, 0) for dy in (2, 1, 3, 0) if dx or dy]

    def remote(src, dst, send, recv, device):
        return pltpu.make_async_remote_copy(
            src_ref=src, dst_ref=dst, send_sem=send, recv_sem=recv,
            device_id=device, device_id_type=pl.DeviceIdType.MESH,
        )

    def push(src, dst, send, recv, device):
        remote(src, dst, send, recv, device).start()

    def arrived(dst, recv):
        remote(dst, dst, ex_s.at[0], recv, sibling).wait_recv()

    def sent_off(src, send):
        remote(src, src, send, ex_r.at[0], sibling).wait_send()

    def offset(s, core):
        return pl.multiple_of(core * PART * s + (1 - core) * (HALF - PART - PART * s), 16)

    own_row = pl.multiple_of(HALF * c, 16)
    other_row = pl.multiple_of(HALF * other, 16)
    line_lane = pl.multiple_of(128 * (z % 4), 128)
    own_block = pl.ds(pl.multiple_of(512 * c, 512), 512)
    other_block = pl.ds(pl.multiple_of(512 * other, 512), 512)
    small = [(bus_price_in, pstage), (marginal_in, prow.at[0:1]), (quad_in, prow.at[1:2]), (cap_in, prow.at[2:3]),
             (width_in, irow.at[0:1]), (bus_in, irow.at[1:2]), (count_in, crow), (dispatch_in, dstage),
             (ramp_in, ramp_v)]
    large = [
        (load_in, ld),
        (ptdf_in, pt.at[own_block]),
        (limit_in.at[pl.ds(own_row, HALF), pl.ds(line_lane, 128)], lim),
        (lp_in.at[pl.ds(own_row, HALF), pl.ds(line_lane, 128)], lps),
    ]
    local = [pltpu.make_async_copy(src, dst, loc.at[i]) for i, (src, dst) in enumerate(small + large)]
    for copy in local:
        copy.start()

    barrier = pltpu.get_barrier_semaphore()
    peers = [sibling]
    peers += [dev(z, chip(*d), c) for d in others]
    peers += [dev((z + d) % 8, g, c) for d in range(1, 8)]
    for peer in peers:
        pl.semaphore_signal(barrier, inc=1, device_id=peer, device_id_type=pl.DeviceIdType.MESH)

    own_lanes = pl.ds(pl.multiple_of(64 * c, 64), 64)
    own_ext = pl.ds(pl.multiple_of(96 * c, 96), EXT)
    other_ext = pl.ds(pl.multiple_of(96 * other, 96), EXT)
    for copy in local[:len(small)]:
        copy.wait()
    stage[...] = jnp.zeros_like(stage)
    stage[own_lanes, 0:H] = pstage[...]
    xp[...] = stage[...].T
    slot = lax.broadcasted_iota(jnp.int32, (1, 64), 1)
    live_row = jnp.where(slot < crow[0:1, 0:1], 1.0, 0.0).astype(F32)
    rows = jnp.concatenate(
        [prow[...], irow[...].astype(F32), live_row, jnp.zeros((2, 64), F32)], axis=0)
    gap = jnp.zeros_like(rows)
    pmo[...] = jnp.where(
        c == 0, jnp.concatenate([rows, gap], axis=1), jnp.concatenate([gap, rows], axis=1))
    pl.semaphore_wait(barrier, len(peers))
    push(pmo, rpm, ex_s.at[1], ex_r.at[1], sibling)
    push(xp.at[pl.ds(other_row, HALF)], rxp, ex_s.at[0], ex_r.at[0], sibling)
    push(ptdf_in, pt.at[own_block], ex_s.at[3], ex_r.at[3], sibling)
    stage[own_lanes, 0:H] = dstage[...]
    xd[...] = stage[...].T
    push(xd.at[other_ext], rxd, ex_s.at[2], ex_r.at[2], sibling)
    push(limit_in.at[pl.ds(other_row, HALF), pl.ds(line_lane, 128)], slim, ex_s.at[4], ex_r.at[4], sibling)
    push(lp_in.at[pl.ds(other_row, HALF), pl.ds(line_lane, 128)], slps, ex_s.at[5], ex_r.at[5], sibling)

    def gather(grid, s, k):
        for d in others:
            push(grid.at[s, g], grid.at[s, g], ag_s.at[k, s], ag_r.at[k, s], dev(z, chip(*d), c))

    def gathered(grid, s, k):
        arrived(grid.at[s, pl.ds(0, 15)], ag_r.at[k, s])
        return jnp.concatenate([grid[s, i] for i in range(16)], axis=1)

    arrived(rpm, ex_r.at[1])
    pm[...] = pmo[...] + rpm[...]
    ids[g] = pm[...]
    for d in others:
        push(ids.at[g], ids.at[g], id_s.at[0], id_r.at[0], dev(z, chip(*d), c))
    arrived(rxp, ex_r.at[0])
    for s in range(PARTS):
        row = offset(s, c)
        mine = xp[pl.ds(pl.multiple_of(own_row + row, 16), PART)]
        ga[s, g] = (mine + rxp[pl.ds(row, PART)]).astype(BF16)
        gather(ga, s, 0)

    for copy in local[len(small):]:
        copy.wait()
    load_all = ld[...].astype(BF16)
    for j in range(2):
        block = pt[pl.ds(pl.multiple_of(512 * c + 256 * j, 256), 256)]
        f0full[j] = lax.dot_general(load_all, block, NT, preferred_element_type=F32)
        f0[2 * c + j] = f0full[j, pl.ds(own_row, HALF)]
    own_pairs = pl.ds(2 * c, 2)
    push(f0full.at[:, pl.ds(other_row, HALF)], f0.at[own_pairs], ex_s.at[11], ex_r.at[11], sibling)

    stage[...] = jnp.zeros_like(stage)
    stage[0:26, 0:H] = ramp_v[...]
    ramp_t[...] = stage[...].T
    marginal, quad, cap, width = (pm[i:i + 1] for i in range(4))
    live = pm[5:6]
    for d in range(0, REACH + 1):
        keep = (width > d - 0.5).astype(F32)
        for o in ((0,) if d == 0 else (d, -d)):
            row = REACH + o
            column = ramp_t[own_ext, row:row + 1]
            if d == 0:
                kt[row] = jnp.broadcast_to(1.0 + column, (EXT, 128))
            else:
                kt[row] = column * keep
    bus_row = lax.broadcasted_iota(jnp.int32, (2048, 128), 0)
    oh[...] = jnp.where(bus_row == pm[4:5].astype(jnp.int32), 1.0, 0.0).astype(BF16)

    arrived(pt.at[other_block], ex_r.at[3])
    arrived(ids.at[pl.ds(0, 15)], id_r.at[0])

    def plant_columns(j, _):
        i = 4 * c + j
        bus = jnp.concatenate([ids[2 * i, 4:5], ids[2 * i + 1, 4:5]], axis=1)
        iota = lax.broadcasted_iota(jnp.int32, (2048, 256), 0)
        one_hot = jnp.where(iota == bus.astype(jnp.int32), 1.0, 0.0).astype(BF16)
        q[i] = jnp.dot(pt[...], one_hot, preferred_element_type=F32).astype(BF16)
        push(q.at[i], q.at[i], q_s.at[j], q_r.at[j], sibling)
        return 0

    core_row = pl.multiple_of(48 * c, 16)
    halo_at = pl.multiple_of(HALF * other, 16)

    def ext_part(s):
        return pl.ds(pl.multiple_of(core_row + offset(s, c), 16), PART)

    def price_part(s):
        px[ext_part(s)] = jnp.dot(gathered(ga, s, 0), oh[...], preferred_element_type=F32)

    lax.fori_loop(0, 2, plant_columns, 0)
    price_part(0)
    halo_s[0] = px[ext_part(0)]
    push(halo_s.at[0], halo_p.at[0], ex_s.at[6], ex_r.at[6], sibling)
    arrived(rxd, ex_r.at[2])
    dsp[...] = xd[own_ext] + rxd[...]
    lax.fori_loop(2, 4, plant_columns, 0)
    price_part(1)
    arrived(slim, ex_r.at[4])
    arrived(slps, ex_r.at[5])
    holds = c == z // 4
    lim[...] = jnp.where(holds, lim[...], slim[...])
    lps[...] = jnp.where(holds, lps[...], slps[...])
    arrived(f0.at[pl.ds(2 * other, 2)], ex_r.at[11])
    vb[...] = jnp.zeros_like(vb)
    arrived(halo_p.at[0], ex_r.at[6])
    px[pl.ds(halo_at, PART)] = halo_p[0]
    price_part(2)

    def sweep(_, carry):
        d = dsp[...]
        vb[16:16 + EXT] = d + 0.5 * (px[...] - marginal - quad * d)
        for r in range(0, EXT, 64):
            total = kt[REACH, r:r + 64] * vb[16 + r:16 + r + 64]
            for s in range(1, REACH + 1):
                for o in (s, -s):
                    total = total + kt[REACH + o, r:r + 64] * vb[16 + o + r:16 + o + r + 64]
            dsp[r:r + 64] = live * jnp.clip(total, 0.0, cap)
        return carry

    def start_gather(k):
        for s in range(PARTS):
            gb[k, s, g] = dsp[ext_part(s)].astype(BF16)
            gather(gb.at[k], s, 1 + k)

    def flow(k, s):
        spread = gathered(gb.at[k], s, 1 + k)
        rows = pl.ds(offset(s, c), PART)
        for dq in (2, 1, 3, 0):
            pair = (z // 2 + dq) % 4
            part = jnp.dot(spread, qt[pair], preferred_element_type=F32) - f0[pair, rows]
            for j in (0, 1):
                fb[k, s, 2 * pair + j] = part[:, 128 * j:128 * j + 128].astype(BF16)
            for j in (0, 1):
                target = 2 * pair + j

                @pl.when(target != z)
                def _():
                    push(fb.at[k, s, target], rc.at[k, s, z], zr_s.at[k, s], zr_r.at[k, s], dev(target, g, c))

    def limit_lines(k, s):
        arrived(rc.at[k, s, pl.ds(0, 7)], zr_r.at[k, s])
        total = fb[k, s, z].astype(F32)
        for d in range(1, 8):
            total = total + rc[k, s, (z + d) % 8].astype(F32)
        rows = pl.ds(offset(s, c), PART)
        shifted = lps[rows] + total
        limit = lim[rows]
        new = shifted - jnp.clip(shifted, -limit, limit)
        lps[rows] = new
        sa[k, s, z] = new.astype(BF16)
        for d in (4, 3, 5, 2, 6, 1, 7):
            push(sa.at[k, s, z], sa.at[k, s, z], zg_s.at[k, s], zg_r.at[k, s], dev((z + d) % 8, g, c))

    def congestion(k, s):
        arrived(sa.at[k, s, pl.ds(0, 7)], zg_r.at[k, s])
        spread = jnp.concatenate([sa[k, s, i] for i in range(8)], axis=1)
        for dx in (2, 1, 3, 0):
            row = (x + dx) % 4
            for h in (0, 1):
                i = 2 * row + h
                matrix = q[i] if k == 0 else pt[:, pl.ds(pl.multiple_of(256 * i, 256), 256)]
                part = jnp.dot(spread, matrix, preferred_element_type=F32).astype(BF16)
                pb[k, s, 2 * i] = part[:, 0:128]
                pb[k, s, 2 * i + 1] = part[:, 128:256]
            for dy in (2, 1, 3, 0):
                if dx or dy:
                    to = chip(dx, dy)
                    push(pb.at[k, s, to], rp.at[k, s, g], rs_s.at[k, s], rs_r.at[k, s], dev(z, to, c))


    def prices(k, s):
        arrived(rp.at[k, s, pl.ds(0, 15)], rs_r.at[k, s])
        total = pb[k, s, g].astype(F32)
        for d in range(1, 16):
            total = total + rp[k, s, (g + d) % 16].astype(F32)
        row = pl.multiple_of(own_row + offset(s, c), 16)
        return ramp_t[pl.ds(row, PART), 25:26] - total

    lax.fori_loop(0, ITERS, sweep, 0)
    start_gather(0)
    halo_s[1] = dsp[ext_part(0)]
    push(halo_s.at[1], halo_d, ex_s.at[7], ex_r.at[7], sibling)
    for j in range(4):
        arrived(q.at[4 * other + j], q_r.at[j])

    def transpose_columns(i, _):
        for pair in range(4):
            qt[pair, pl.ds(pl.multiple_of(256 * i, 256), 256)] = q[i, 256 * pair:256 * pair + 256].T
        return 0

    lax.fori_loop(0, 8, transpose_columns, 0)
    for s in range(PARTS):
        flow(0, s)
    for s in range(PARTS):
        limit_lines(0, s)
    for s in range(PARTS):
        congestion(0, s)
    for s in range(PARTS):
        px[ext_part(s)] = prices(0, s)
        if s == 0:
            halo_s[2] = px[ext_part(0)]
            push(halo_s.at[2], halo_p.at[1], ex_s.at[8], ex_r.at[8], sibling)
            arrived(halo_d, ex_r.at[7])
            dsp[pl.ds(halo_at, PART)] = halo_d[...]
    arrived(halo_p.at[1], ex_r.at[8])
    px[pl.ds(halo_at, PART)] = halo_p[1]

    lax.fori_loop(0, ITERS, sweep, 0)
    start_gather(1)
    fd_s[...] = dsp[pl.ds(core_row, HALF)]
    push(fd_s, fd_r, ex_s.at[9], ex_r.at[9], sibling)

    def rows_out(mine, theirs):
        gap = jnp.zeros((96, 128), F32)
        first = jnp.where(c == 0, mine, theirs)
        second = jnp.where(c == 0, theirs, mine)
        return jnp.concatenate([first, second, gap], axis=0).T

    arrived(fd_r, ex_r.at[9])
    stage[...] = rows_out(fd_s[...], fd_r[...])
    dispatch_out[...] = stage[own_lanes, 0:H]
    for s in range(PARTS):
        flow(1, s)
    for s in range(PARTS):
        limit_lines(1, s)
    for s in range(PARTS):
        congestion(1, s)
    push(sa.at[1, :, pl.ds(pl.multiple_of(4 * other, 4), 4)], lr, ex_s.at[10], ex_r.at[10], sibling)
    for s in range(PARTS):
        rows = pl.ds(pl.multiple_of(own_row + offset(s, c), 16), PART)
        for i in range(4):
            line_out[rows, 128 * i:128 * i + 128] = sa[1, s, 4 * c + i].astype(F32)
    for s in range(PARTS):
        rows = pl.ds(offset(s, c), PART)
        fin_s[rows] = prices(1, s)
        push(fin_s.at[rows], fin_r.at[rows], ex_s.at[12 + s], ex_r.at[12 + s], sibling)
    arrived(lr, ex_r.at[10])
    for s in range(PARTS):
        rows = pl.ds(pl.multiple_of(other_row + offset(s, other), 16), PART)
        for i in range(4):
            line_out[rows, 128 * i:128 * i + 128] = lr[s, i].astype(F32)
    for s in range(PARTS):
        arrived(fin_r.at[pl.ds(offset(s, other), PART)], ex_r.at[12 + s])
    stage[...] = rows_out(fin_s[...], fin_r[...])
    bus_out[...] = stage[own_lanes, 0:H]

    for ref, i in ((pmo, 1), (rxp, 0), (ptdf_in, 3), (rxd, 2), (slim, 4), (slps, 5), (f0.at[own_pairs], 11),
                   (halo_s.at[0], 6), (halo_s.at[1], 7), (halo_s.at[2], 8), (fd_s, 9), (lr, 10),
                   (fin_s.at[0:PART], 12), (fin_s.at[0:PART], 13), (fin_s.at[0:PART], 14)):
        sent_off(ref, ex_s.at[i])
    sent_off(ids.at[pl.ds(0, 15)], id_s.at[0])
    for j in range(4):
        sent_off(q.at[j], q_s.at[j])
    for s in range(PARTS):
        for k in range(3):
            sent_off(ga.at[s, pl.ds(0, 15), pl.ds(0, PART)], ag_s.at[k, s])
        for k in range(2):
            sent_off(rc.at[k, s, pl.ds(0, 7)], zr_s.at[k, s])
            sent_off(sa.at[k, s, pl.ds(0, 7)], zg_s.at[k, s])
            sent_off(rp.at[k, s, pl.ds(0, 15)], rs_s.at[k, s])


def shards(
    dispatch_start, marginal_cost, quad_cost, capacity, band_widths, ramp_band, plant_bus, plant_counts,
    load, ptdf, line_limit, line_price_start, bus_price_start, energy_price,
):
    ramp = jnp.concatenate([ramp_band, energy_price[None]], axis=0)
    vmem = pl.BlockSpec(memory_space=pltpu.VMEM)
    hbm = pl.BlockSpec(memory_space=pltpu.HBM)
    sem = pltpu.SemaphoreType.DMA

    def v(shape, kind=F32):
        return pltpu.VMEM(shape, kind)

    scratch = [
        v((64, H)), v((64, H)), v((3, 64)), v((2, 64), jnp.int32), v((1, 1), jnp.int32), v((26, H)),
        v((128, 384)), v((384, 128)), v((384, 128)), v((EXT, 128)), v((HALF, 128)),
        v((8, 128)), v((8, 128)), v((8, 128)), v((16, 8, 128)),
        v((384, 128)), v((25, EXT, 128)), v((EXT + 32, 128)), v((EXT, 128)), v((EXT, 128)),
        v((2048, 128), BF16),
        v((1024, 2048), BF16), v((8, 1024, 256), BF16), v((4, 2048, 256), BF16), v((H, 2048)),
        v((HALF, 128)), v((HALF, 128)), v((HALF, 128)), v((HALF, 128)),
        v((4, HALF, 256)), v((2, H, 256)),
        v((PARTS, 16, PART, 128), BF16), v((2, PARTS, 16, PART, 128), BF16),
        v((2, PARTS, 8, PART, 128), BF16), v((2, PARTS, 8, PART, 128), BF16),
        v((2, PARTS, 8, PART, 128), BF16),
        v((2, PARTS, 16, PART, 128), BF16), v((2, PARTS, 16, PART, 128), BF16),
        v((3, PART, 128)), v((2, PART, 128)), v((PART, 128)),
        v((HALF, 128)), v((HALF, 128)), v((HALF, 128)), v((HALF, 128)),
        v((PARTS, 4, PART, 128), BF16),
        sem((13,)), sem((15,)), sem((15,)), sem((1,)), sem((1,)), sem((4,)), sem((4,)),
        sem((3, PARTS)), sem((3, PARTS)), sem((2, PARTS)), sem((2, PARTS)), sem((2, PARTS)), sem((2, PARTS)),
        sem((2, PARTS)), sem((2, PARTS)),
    ]
    dispatch, line_price, bus_price = pl.pallas_call(
        body,
        out_shape=(
            jax.ShapeDtypeStruct((64, H), F32),
            jax.ShapeDtypeStruct((H, 512), F32),
            jax.ShapeDtypeStruct((64, H), F32),
        ),
        in_specs=[hbm] * 13,
        out_specs=(vmem,) * 3,
        scratch_shapes=scratch,
        compiler_params=pltpu.CompilerParams(
            collective_id=0, has_side_effects=True, vmem_limit_bytes=56 * 2**20),
        name="dispatch_window",
    )(
        dispatch_start, bus_price_start, marginal_cost[None], quad_cost[None], capacity[None],
        band_widths[None], plant_bus[None], plant_counts[None], ramp, load.T, ptdf, line_limit.T,
        line_price_start.T,
    )
    return dispatch, line_price.T, bus_price


def solution(mesh):
    placed = (
        P(("region", "plant"), None),
        P(("region", "plant")),
        P(("region", "plant")),
        P(("region", "plant")),
        P(("region", "plant")),
        P(),
        P(("region", "plant")),
        P(("region", "plant")),
        P("region", None),
        P("plant", "region"),
        P("plant", None),
        P("plant", None),
        P(("region", "plant"), None),
        P(),
    )
    return jax.shard_map(
        shards,
        mesh=mesh,
        in_specs=placed,
        out_specs=(P(("region", "plant"), None), P("plant", None), P(("region", "plant"), None)),
        check_vma=False,
    )
```

```python
import jax
import jax.numpy as jnp
from jax import lax
from jax.experimental import pallas as pl
from jax.experimental.pallas import tpu as pltpu
from jax.sharding import PartitionSpec as P

H = 288
HALF = 144
EXT = 192
PARTS = 3
PART = 48
REACH = 12
ITERS = 3
F32 = jnp.float32
BF16 = jnp.bfloat16
NN = (((1,), (0,)), ((), ()))
NT = (((1,), (1,)), ((), ()))
FAR_FIRST = (2, 1, 3)


def body(
    dispatch_in, bus_price_in, marginal_in, quad_in, cap_in, width_in, bus_in, count_in, ramp_in, energy_in,
    load_in, ptdf_in, limit_in, lp_in,
    dispatch_out, line_out, bus_out,
    dboth, pboth, prow, irow, crow, ramp_v, energy_v, stage, xd, xp, pm, ids, ramp_t, kt, vb, dsp, px, oh,
    pt, q, qt, ld, lim, lps, slim, slps, f0, f0full,
    ga, gb, fb, rc, sa, pb, rp,
    vbe, dse, halo_s, halo_p, halo_d, fin_s, fin_r, fd_s, fd_r, lr,
    loc, ex_s, ex_r, cr_s, cr_r, id_s, id_r, q_s, q_r, ag_s, ag_r, zr_s, zr_r, zg_s, zg_r, rs_s, rs_r,
):
    z = lax.axis_index("region")
    p = lax.axis_index("plant")
    g = p // 2
    x = g // 4
    y = g % 4
    c = p % 2
    other = 1 - c
    no = z // 8

    def dev(zz, gg, cc):
        return (zz, gg * 2 + cc)

    sibling = dev(z, g, other)

    def chip(dx, dy):
        return ((x + dx) % 4) * 4 + (y + dy) % 4

    others = [(dx, dy) for dx in (2, 1, 3, 0) for dy in (2, 1, 3, 0) if dx or dy]

    def remote(src, dst, send, recv, device):
        return pltpu.make_async_remote_copy(
            src_ref=src, dst_ref=dst, send_sem=send, recv_sem=recv,
            device_id=device, device_id_type=pl.DeviceIdType.MESH,
        )

    def push(src, dst, send, recv, device):
        remote(src, dst, send, recv, device).start()

    def arrived(dst, recv):
        remote(dst, dst, ex_s.at[0], recv, sibling).wait_recv()

    def sent_off(src, send):
        remote(src, src, send, ex_r.at[0], sibling).wait_send()

    def offset(s, core):
        return pl.multiple_of(core * PART * s + (1 - core) * (HALF - PART - PART * s), 16)

    own_row = pl.multiple_of(HALF * c, 16)
    other_row = pl.multiple_of(HALF * other, 16)
    line_lane = pl.multiple_of(128 * (z % 4), 128)
    own_block = pl.ds(pl.multiple_of(512 * c, 512), 512)
    other_block = pl.ds(pl.multiple_of(512 * other, 512), 512)
    own_lanes = pl.ds(pl.multiple_of(64 * c, 64), 64)
    rows_in = [(marginal_in, 0), (quad_in, 1), (cap_in, 2)]
    cores = [
        (bus_price_in, pboth.at[own_lanes]),
        *[(ref, prow.at[c, i:i + 1]) for ref, i in rows_in],
        (width_in, irow.at[c, 0:1]), (bus_in, irow.at[c, 1:2]), (count_in, crow.at[c]),
        (dispatch_in, dboth.at[own_lanes]),
    ]
    other_lanes = pl.ds(pl.multiple_of(64 * other, 64), 64)
    cores_other = [pboth.at[other_lanes], *[prow.at[other, i:i + 1] for i in range(3)],
                   irow.at[other, 0:1], irow.at[other, 1:2], crow.at[other], dboth.at[other_lanes]]
    small = cores + [(ramp_in, ramp_v), (energy_in, energy_v)]
    large = [
        (load_in, ld),
        (ptdf_in, pt.at[own_block]),
        (limit_in.at[pl.ds(own_row, HALF), pl.ds(line_lane, 128)], lim),
        (lp_in.at[pl.ds(own_row, HALF), pl.ds(line_lane, 128)], lps),
    ]
    local = [pltpu.make_async_copy(src, dst, loc.at[i]) for i, (src, dst) in enumerate(small + large)]
    for copy in local:
        copy.start()

    barrier = pltpu.get_barrier_semaphore()
    peers = [sibling]
    peers += [dev(z, chip(*d), c) for d in others]
    peers += [dev((z + d) % 8, g, c) for d in range(1, 8)]
    for peer in peers:
        pl.semaphore_signal(barrier, inc=1, device_id=peer, device_id_type=pl.DeviceIdType.MESH)

    own_ext = pl.ds(pl.multiple_of(96 * c, 96), EXT)
    pl.semaphore_wait(barrier, len(peers))
    for i, (src, dst) in enumerate(cores):
        push(src, dst, cr_s.at[i], cr_r.at[i], sibling)
    push(ptdf_in, pt.at[own_block], ex_s.at[3], ex_r.at[3], sibling)
    push(limit_in.at[pl.ds(other_row, HALF), pl.ds(line_lane, 128)], slim, ex_s.at[4], ex_r.at[4], sibling)
    push(lp_in.at[pl.ds(other_row, HALF), pl.ds(line_lane, 128)], slps, ex_s.at[5], ex_r.at[5], sibling)

    def gather(grid, s, k):
        for d in others:
            push(grid.at[s, g], grid.at[s, g], ag_s.at[k, s], ag_r.at[k, s], dev(z, chip(*d), c))

    def gathered(grid, s, k):
        arrived(grid.at[s, pl.ds(0, 15)], ag_r.at[k, s])
        return jnp.concatenate([grid[s, i] for i in range(16)], axis=1)

    for copy in local[:len(small)]:
        copy.wait()
    for i in range(1, 7):
        arrived(cores_other[i], cr_r.at[i])
    slot = lax.broadcasted_iota(jnp.int32, (1, 64), 1)
    pm[...] = jnp.concatenate([
        jnp.concatenate([
            prow[i], irow[i].astype(F32), jnp.where(slot < crow[i], 1.0, 0.0).astype(F32),
            jnp.zeros((2, 64), F32),
        ], axis=0) for i in (0, 1)], axis=1)
    ids[g] = pm[...]
    for d in others:
        push(ids.at[g], ids.at[g], id_s.at[0], id_r.at[0], dev(z, chip(*d), c))
    arrived(cores_other[0], cr_r.at[0])
    stage[...] = jnp.zeros_like(stage)
    stage[:, 0:H] = pboth[...]
    xp[...] = stage[...].T
    for s in range(PARTS):
        ga[s, g] = xp[pl.ds(pl.multiple_of(own_row + offset(s, c), 16), PART)].astype(BF16)
        gather(ga, s, 0)

    for copy in local[len(small):]:
        copy.wait()
    load_all = ld[...].astype(BF16)
    for j in range(2):
        block = pt[pl.ds(pl.multiple_of(512 * c + 256 * j, 256), 256)]
        f0full[j] = lax.dot_general(load_all, block, NT, preferred_element_type=F32)
        f0[2 * c + j] = f0full[j, pl.ds(own_row, HALF)]
    own_pairs = pl.ds(2 * c, 2)
    push(f0full.at[:, pl.ds(other_row, HALF)], f0.at[own_pairs], ex_s.at[11], ex_r.at[11], sibling)

    stage[...] = jnp.zeros_like(stage)
    stage[0:25, 0:H] = ramp_v[...]
    stage[25:26, 0:H] = energy_v[...].reshape(1, H)
    ramp_t[...] = stage[...].T
    marginal, quad, cap, width = (pm[i:i + 1] for i in range(4))
    live = pm[5:6]
    for d in range(0, REACH + 1):
        keep = (width > d - 0.5).astype(F32)
        for o in ((0,) if d == 0 else (d, -d)):
            row = REACH + o
            column = ramp_t[own_ext, row:row + 1]
            if d == 0:
                kt[row] = jnp.broadcast_to(1.0 + column, (EXT, 128))
            else:
                kt[row] = column * keep
    bus_row = lax.broadcasted_iota(jnp.int32, (2048, 128), 0)
    oh[...] = jnp.where(bus_row == pm[4:5].astype(jnp.int32), 1.0, 0.0).astype(BF16)

    arrived(pt.at[other_block], ex_r.at[3])
    arrived(ids.at[pl.ds(0, 15)], id_r.at[0])

    def plant_columns(j, _):
        i = 4 * c + j
        bus = jnp.concatenate([ids[2 * i, 4:5], ids[2 * i + 1, 4:5]], axis=1)
        iota = lax.broadcasted_iota(jnp.int32, (2048, 256), 0)
        one_hot = jnp.where(iota == bus.astype(jnp.int32), 1.0, 0.0).astype(BF16)
        q[i] = jnp.dot(pt[...], one_hot, preferred_element_type=F32).astype(BF16)
        push(q.at[i], q.at[i], q_s.at[j], q_r.at[j], sibling)
        return 0

    core_row = pl.multiple_of(48 * c, 16)
    halo_at = pl.multiple_of(HALF * other, 16)

    def ext_part(s):
        return pl.ds(pl.multiple_of(core_row + offset(s, c), 16), PART)

    def price_part(s):
        px[ext_part(s)] = jnp.dot(gathered(ga, s, 0), oh[...], preferred_element_type=F32)

    vb[...] = jnp.zeros_like(vb)
    vbe[...] = jnp.zeros_like(vbe)
    lax.fori_loop(0, 2, plant_columns, 0)
    price_part(0)
    halo_s[0] = px[ext_part(0)]
    push(halo_s.at[0], halo_p.at[0], ex_s.at[6], ex_r.at[6], sibling)
    arrived(cores_other[7], cr_r.at[7])
    stage[:, 0:H] = dboth[...]
    xd[...] = stage[...].T
    dsp[...] = xd[own_ext]
    def sweep(_, carry):
        d = dsp[...]
        vb[16:16 + EXT] = d + 0.5 * (px[...] - marginal - quad * d)
        for r in range(0, EXT, 64):
            total = kt[REACH, r:r + 64] * vb[16 + r:16 + r + 64]
            for s in range(1, REACH + 1):
                for o in (s, -s):
                    total = total + kt[REACH + o, r:r + 64] * vb[16 + o + r:16 + o + r + 64]
            dsp[r:r + 64] = live * jnp.clip(total, 0.0, cap)
        return carry

    early_row = pl.multiple_of(48 * other, 16)

    def early_part(k):
        rows = pl.ds(early_row, HALF)
        price = px[rows]
        dse[...] = dsp[rows]

        def step(_, carry):
            d = dse[...]
            vbe[16:16 + HALF] = d + 0.5 * (price - marginal - quad * d)
            for r in range(0, HALF, PART):
                at = pl.ds(pl.multiple_of(early_row + r, 16), PART)
                total = kt[REACH, at] * vbe[16 + r:16 + r + PART]
                for s in range(1, REACH + 1):
                    for o in (s, -s):
                        total = total + kt[REACH + o, at] * vbe[16 + o + r:16 + o + r + PART]
                dse[r:r + PART] = live * jnp.clip(total, 0.0, cap)
            return carry

        lax.fori_loop(0, ITERS, step, 0)
        gb[k, 0, g] = dse[PART:2 * PART].astype(BF16)
        gather(gb.at[k], 0, 1 + k)

    def other_parts(k):
        for s in range(1, PARTS):
            gb[k, s, g] = dsp[ext_part(s)].astype(BF16)
            gather(gb.at[k], s, 1 + k)

    def flow(k, s):
        spread = gathered(gb.at[k], s, 1 + k)
        rows = pl.ds(offset(s, c), PART)
        for dq in (2, 1, 3, 0):
            pair = (z // 2 + dq) % 4
            part = jnp.dot(spread, qt[pair], preferred_element_type=F32) - f0[pair, rows]
            for j in (0, 1):
                fb[k, s, 2 * pair + j] = part[:, 128 * j:128 * j + 128].astype(BF16)
            for j in (0, 1):
                target = 2 * pair + j

                @pl.when(target != z)
                def _():
                    push(fb.at[k, s, target], rc.at[k, s, z], zr_s.at[k, s], zr_r.at[k, s], dev(target, g, c))

    def limit_lines(k, s):
        arrived(rc.at[k, s, pl.ds(0, 7)], zr_r.at[k, s])
        total = fb[k, s, z].astype(F32)
        for d in range(1, 8):
            total = total + rc[k, s, (z + d) % 8].astype(F32)
        rows = pl.ds(offset(s, c), PART)
        shifted = lps[rows] + total
        limit = lim[rows]
        new = shifted - jnp.clip(shifted, -limit, limit)
        lps[rows] = new
        sa[k, s, z] = new.astype(BF16)
        for d in (4, 3, 5, 2, 6, 1, 7):
            push(sa.at[k, s, z], sa.at[k, s, z], zg_s.at[k, s], zg_r.at[k, s], dev((z + d) % 8, g, c))

    def congestion(k, s):
        arrived(sa.at[k, s, pl.ds(0, 7)], zg_r.at[k, s])
        spread = jnp.concatenate([sa[k, s, i] for i in range(8)], axis=1)
        for dx in (2, 1, 3, 0):
            row = (x + dx) % 4
            for h in (0, 1):
                i = 2 * row + h
                matrix = q[i] if k == 0 else pt[:, pl.ds(pl.multiple_of(256 * i, 256), 256)]
                part = jnp.dot(spread, matrix, preferred_element_type=F32).astype(BF16)
                pb[k, s, 2 * i] = part[:, 0:128]
                pb[k, s, 2 * i + 1] = part[:, 128:256]
            for dy in (2, 1, 3, 0):
                if dx or dy:
                    to = chip(dx, dy)
                    push(pb.at[k, s, to], rp.at[k, s, g], rs_s.at[k, s], rs_r.at[k, s], dev(z, to, c))


    def prices(k, s):
        arrived(rp.at[k, s, pl.ds(0, 15)], rs_r.at[k, s])
        total = pb[k, s, g].astype(F32)
        for d in range(1, 16):
            total = total + rp[k, s, (g + d) % 16].astype(F32)
        row = pl.multiple_of(own_row + offset(s, c), 16)
        return ramp_t[pl.ds(row, PART), 25:26] - total

    lax.fori_loop(2, 3 + no, plant_columns, 0)
    price_part(1)
    arrived(halo_p.at[0], ex_r.at[6])
    px[pl.ds(halo_at, PART)] = halo_p[0]
    early_part(0)
    price_part(2)
    lax.fori_loop(0, ITERS, sweep, 0)
    other_parts(0)
    halo_s[1] = dsp[ext_part(0)]
    push(halo_s.at[1], halo_d, ex_s.at[7], ex_r.at[7], sibling)
    lax.fori_loop(3, 4 + no, plant_columns, 0)
    arrived(slim, ex_r.at[4])
    arrived(slps, ex_r.at[5])
    holds = c == z // 4
    lim[...] = jnp.where(holds, lim[...], slim[...])
    lps[...] = jnp.where(holds, lps[...], slps[...])
    arrived(f0.at[pl.ds(2 * other, 2)], ex_r.at[11])

    def transpose_columns(j, core):
        i = 4 * core + j
        for pair in range(4):
            qt[pair, pl.ds(pl.multiple_of(256 * i, 256), 256)] = q[i, 256 * pair:256 * pair + 256].T
        return core

    lax.fori_loop(0, 4, transpose_columns, c)
    for j in range(4):
        arrived(q.at[4 * other + j], q_r.at[j])
    lax.fori_loop(0, 4, transpose_columns, other)
    for s in range(PARTS):
        flow(0, s)
    for s in range(PARTS):
        limit_lines(0, s)
    for s in range(PARTS):
        congestion(0, s)
    px[ext_part(0)] = prices(0, 0)
    halo_s[2] = px[ext_part(0)]
    push(halo_s.at[2], halo_p.at[1], ex_s.at[8], ex_r.at[8], sibling)
    arrived(halo_d, ex_r.at[7])
    dsp[pl.ds(halo_at, PART)] = halo_d[...]
    px[ext_part(1)] = prices(0, 1)
    arrived(halo_p.at[1], ex_r.at[8])
    px[pl.ds(halo_at, PART)] = halo_p[1]

    early_part(1)
    px[ext_part(2)] = prices(0, 2)
    lax.fori_loop(0, ITERS, sweep, 0)
    other_parts(1)
    fd_s[...] = dsp[pl.ds(core_row, HALF)]
    push(fd_s, fd_r, ex_s.at[9], ex_r.at[9], sibling)

    def rows_out(mine, theirs):
        gap = jnp.zeros((96, 128), F32)
        first = jnp.where(c == 0, mine, theirs)
        second = jnp.where(c == 0, theirs, mine)
        return jnp.concatenate([first, second, gap], axis=0).T

    arrived(fd_r, ex_r.at[9])
    stage[...] = rows_out(fd_s[...], fd_r[...])
    dispatch_out[...] = stage[own_lanes, 0:H]
    for s in range(PARTS):
        flow(1, s)
    for s in range(PARTS):
        limit_lines(1, s)
    for s in range(PARTS):
        congestion(1, s)
    push(sa.at[1, :, pl.ds(pl.multiple_of(4 * other, 4), 4)], lr, ex_s.at[10], ex_r.at[10], sibling)
    for s in range(PARTS):
        rows = pl.ds(pl.multiple_of(own_row + offset(s, c), 16), PART)
        for i in range(4):
            line_out[rows, 128 * i:128 * i + 128] = sa[1, s, 4 * c + i].astype(F32)
    for s in range(PARTS):
        rows = pl.ds(offset(s, c), PART)
        fin_s[rows] = prices(1, s)
        push(fin_s.at[rows], fin_r.at[rows], ex_s.at[12 + s], ex_r.at[12 + s], sibling)
    arrived(lr, ex_r.at[10])
    for s in range(PARTS):
        rows = pl.ds(pl.multiple_of(other_row + offset(s, other), 16), PART)
        for i in range(4):
            line_out[rows, 128 * i:128 * i + 128] = lr[s, i].astype(F32)
    for s in range(PARTS):
        arrived(fin_r.at[pl.ds(offset(s, other), PART)], ex_r.at[12 + s])
    stage[...] = rows_out(fin_s[...], fin_r[...])
    bus_out[...] = stage[own_lanes, 0:H]

    for i, (ref, _) in enumerate(cores):
        sent_off(ref, cr_s.at[i])
    for ref, i in ((ptdf_in, 3), (slim, 4), (slps, 5), (f0.at[own_pairs], 11),
                   (halo_s.at[0], 6), (halo_s.at[1], 7), (halo_s.at[2], 8), (fd_s, 9), (lr, 10),
                   (fin_s.at[0:PART], 12), (fin_s.at[0:PART], 13), (fin_s.at[0:PART], 14)):
        sent_off(ref, ex_s.at[i])
    sent_off(ids.at[pl.ds(0, 15)], id_s.at[0])
    for j in range(4):
        sent_off(q.at[j], q_s.at[j])
    for s in range(PARTS):
        for k in range(3):
            sent_off(ga.at[s, pl.ds(0, 15), pl.ds(0, PART)], ag_s.at[k, s])
        for k in range(2):
            sent_off(rc.at[k, s, pl.ds(0, 7)], zr_s.at[k, s])
            sent_off(sa.at[k, s, pl.ds(0, 7)], zg_s.at[k, s])
            sent_off(rp.at[k, s, pl.ds(0, 15)], rs_s.at[k, s])


def shards(
    dispatch_start, marginal_cost, quad_cost, capacity, band_widths, ramp_band, plant_bus, plant_counts,
    load, ptdf, line_limit, line_price_start, bus_price_start, energy_price,
):
    vmem = pl.BlockSpec(memory_space=pltpu.VMEM)
    hbm = pl.BlockSpec(memory_space=pltpu.HBM)
    sem = pltpu.SemaphoreType.DMA

    def in_hbm(array):
        return pltpu.with_memory_space_constraint(array, pltpu.HBM)

    def v(shape, kind=F32):
        return pltpu.VMEM(shape, kind)

    scratch = [
        v((128, H)), v((128, H)), v((2, 3, 64)), v((2, 2, 64), jnp.int32), v((2, 1, 1), jnp.int32), v((25, H)), v((H,)),
        v((128, 384)), v((384, 128)), v((384, 128)), v((8, 128)), v((16, 8, 128)),
        v((384, 128)), v((25, EXT, 128)), v((EXT + 32, 128)), v((EXT, 128)), v((EXT, 128)),
        v((2048, 128), BF16),
        v((1024, 2048), BF16), v((8, 1024, 256), BF16), v((4, 2048, 256), BF16), v((H, 2048)),
        v((HALF, 128)), v((HALF, 128)), v((HALF, 128)), v((HALF, 128)),
        v((4, HALF, 256)), v((2, H, 256)),
        v((PARTS, 16, PART, 128), BF16), v((2, PARTS, 16, PART, 128), BF16),
        v((2, PARTS, 8, PART, 128), BF16), v((2, PARTS, 8, PART, 128), BF16),
        v((2, PARTS, 8, PART, 128), BF16),
        v((2, PARTS, 16, PART, 128), BF16), v((2, PARTS, 16, PART, 128), BF16),
        v((HALF + 32, 128)), v((HALF, 128)),
        v((3, PART, 128)), v((2, PART, 128)), v((PART, 128)),
        v((HALF, 128)), v((HALF, 128)), v((HALF, 128)), v((HALF, 128)),
        v((PARTS, 4, PART, 128), BF16),
        sem((14,)), sem((15,)), sem((15,)), sem((8,)), sem((8,)), sem((1,)), sem((1,)), sem((4,)), sem((4,)),
        sem((3, PARTS)), sem((3, PARTS)), sem((2, PARTS)), sem((2, PARTS)), sem((2, PARTS)), sem((2, PARTS)),
        sem((2, PARTS)), sem((2, PARTS)),
    ]
    dispatch, line_price, bus_price = pl.pallas_call(
        body,
        out_shape=(
            jax.ShapeDtypeStruct((64, H), F32),
            jax.ShapeDtypeStruct((H, 512), F32),
            jax.ShapeDtypeStruct((64, H), F32),
        ),
        in_specs=[hbm] * 14,
        out_specs=(vmem,) * 3,
        scratch_shapes=scratch,
        compiler_params=pltpu.CompilerParams(
            collective_id=0, has_side_effects=True, vmem_limit_bytes=40 * 2**20),
        name="dispatch_window",
    )(
        *map(in_hbm, (dispatch_start, bus_price_start, marginal_cost[None], quad_cost[None], capacity[None],
                      band_widths[None], plant_bus[None])),
        plant_counts[None],
        *map(in_hbm, (ramp_band, energy_price, load.T, ptdf, line_limit.T, line_price_start.T)),
    )
    return dispatch, line_price.T, bus_price


def solution(mesh):
    placed = (
        P(("region", "plant"), None),
        P(("region", "plant")),
        P(("region", "plant")),
        P(("region", "plant")),
        P(("region", "plant")),
        P(),
        P(("region", "plant")),
        P(("region", "plant")),
        P("region", None),
        P("plant", "region"),
        P("plant", None),
        P("plant", None),
        P(("region", "plant"), None),
        P(),
    )
    return jax.shard_map(
        shards,
        mesh=mesh,
        in_specs=placed,
        out_specs=(P(("region", "plant"), None), P("plant", None), P(("region", "plant"), None)),
        check_vma=False,
    )
```

```python
import jax
import jax.numpy as jnp
from jax import lax
from jax.experimental import pallas as pl
from jax.experimental.pallas import tpu as pltpu
from jax.sharding import PartitionSpec as P

H = 288
HALF = 144
EXT = 192
SIZES = (48, 48, 48)
STARTS = (0, 48, 96)
PARTS = len(SIZES)
MOST = max(SIZES)
HALO = 48
REACH = 12
ITERS = 3
F32 = jnp.float32
BF16 = jnp.bfloat16
NN = (((1,), (0,)), ((), ()))
NT = (((1,), (1,)), ((), ()))
FAR_FIRST = (2, 1, 3)


def body(
    dispatch_in, bus_price_in, marginal_in, quad_in, cap_in, width_in, bus_in, count_in, ramp_in, energy_in,
    load_in, ptdf_in, limit_in, lp_in,
    both_out, line_out,
    dboth, pboth, prow, irow, crow, ramp_v, energy_v, stage, xd, xp, pm, ids, ramp_t, kt, vb, dsp, px, oh,
    pt, q, qt, ld, lim, lps, slim, slps, f0, f0full,
    ga, gb, fb, rc, sa, pb, rp,
    vbe, dse, halo_s, halo_p, halo_d, fin_s, fin_r, fd_s, fd_r, lr,
    loc, ex_s, ex_r, lr_s, lr_r, fin_ss, fin_rs, cr_s, cr_r, id_s, id_r, q_s, q_r, ag_s, ag_r, zr_s, zr_r, zg_s, zg_r, rs_s, rs_r,
):
    z = lax.axis_index("region")
    p = lax.axis_index("plant")
    g = p // 2
    x = g // 4
    y = g % 4
    c = p % 2
    other = 1 - c
    no = z // 8

    def dev(zz, gg, cc):
        return (zz, gg * 2 + cc)

    sibling = dev(z, g, other)

    def chip(dx, dy):
        return ((x + dx) % 4) * 4 + (y + dy) % 4

    others = [(dx, dy) for dy in (2, 1, 3, 0) for dx in (2, 1, 3, 0) if dx or dy]

    def remote(src, dst, send, recv, device):
        return pltpu.make_async_remote_copy(
            src_ref=src, dst_ref=dst, send_sem=send, recv_sem=recv,
            device_id=device, device_id_type=pl.DeviceIdType.MESH,
        )

    def push(src, dst, send, recv, device):
        remote(src, dst, send, recv, device).start()

    def arrived(dst, recv):
        remote(dst, dst, ex_s.at[0], recv, sibling).wait_recv()

    def sent_off(src, send):
        remote(src, src, send, ex_r.at[0], sibling).wait_send()

    def offset(s, core):
        return pl.multiple_of(core * STARTS[s] + (1 - core) * (HALF - STARTS[s] - SIZES[s]), 16)

    own_row = pl.multiple_of(HALF * c, 16)
    other_row = pl.multiple_of(HALF * other, 16)
    line_lane = pl.multiple_of(128 * (z % 4), 128)
    own_block = pl.ds(pl.multiple_of(512 * c, 512), 512)
    other_block = pl.ds(pl.multiple_of(512 * other, 512), 512)
    own_lanes = pl.ds(pl.multiple_of(64 * c, 64), 64)
    rows_in = [(marginal_in, 0), (quad_in, 1), (cap_in, 2)]
    cores = [
        (bus_price_in, pboth.at[own_lanes]),
        *[(ref, prow.at[c, i:i + 1]) for ref, i in rows_in],
        (width_in, irow.at[c, 0:1]), (bus_in, irow.at[c, 1:2]), (count_in, crow.at[c]),
        (dispatch_in, dboth.at[own_lanes]),
    ]
    other_lanes = pl.ds(pl.multiple_of(64 * other, 64), 64)
    cores_other = [pboth.at[other_lanes], *[prow.at[other, i:i + 1] for i in range(3)],
                   irow.at[other, 0:1], irow.at[other, 1:2], crow.at[other], dboth.at[other_lanes]]
    small = cores + [(ramp_in, ramp_v), (energy_in, energy_v)]
    large = [
        (load_in, ld),
        (ptdf_in, pt.at[own_block]),
        (limit_in.at[pl.ds(own_row, HALF), pl.ds(line_lane, 128)], lim),
        (lp_in.at[pl.ds(own_row, HALF), pl.ds(line_lane, 128)], lps),
    ]
    local = [pltpu.make_async_copy(src, dst, loc.at[i]) for i, (src, dst) in enumerate(small + large)]
    for copy in local:
        copy.start()

    barrier = pltpu.get_barrier_semaphore()
    peers = [sibling]
    peers += [dev(z, chip(*d), core) for d in others for core in (c, other)]
    peers += [dev((z + d) % 8, g, c) for d in range(1, 8)]
    for peer in peers:
        pl.semaphore_signal(barrier, inc=1, device_id=peer, device_id_type=pl.DeviceIdType.MESH)

    own_ext = pl.ds(pl.multiple_of(96 * c, 96), EXT)
    pl.semaphore_wait(barrier, len(peers))
    for i, (src, dst) in enumerate(cores):
        push(src, dst, cr_s.at[i], cr_r.at[i], sibling)
    for d in others:
        for core in (c, other):
            push(bus_in, ids.at[g, c], id_s.at[0], id_r.at[0], dev(z, chip(*d), core))
    push(ptdf_in, pt.at[own_block], ex_s.at[3], ex_r.at[3], sibling)
    push(limit_in.at[pl.ds(other_row, HALF), pl.ds(line_lane, 128)], slim, ex_s.at[4], ex_r.at[4], sibling)
    push(lp_in.at[pl.ds(other_row, HALF), pl.ds(line_lane, 128)], slps, ex_s.at[5], ex_r.at[5], sibling)

    def gather(grid, s, k):
        for d in others:
            block = grid.at[s, g, pl.ds(0, SIZES[s])]
            push(block, block, ag_s.at[k, s], ag_r.at[k, s], dev(z, chip(*d), c))

    def gathered(grid, s, k):
        arrived(grid.at[s, pl.ds(0, 15), pl.ds(0, SIZES[s])], ag_r.at[k, s])
        return jnp.concatenate([grid[s, i, 0:SIZES[s]] for i in range(16)], axis=1)

    for copy in local[:len(small)]:
        copy.wait()
    for i in range(1, 7):
        arrived(cores_other[i], cr_r.at[i])
    slot = lax.broadcasted_iota(jnp.int32, (1, 64), 1)
    pm[...] = jnp.concatenate([
        jnp.concatenate([
            prow[i], irow[i].astype(F32), jnp.where(slot < crow[i], 1.0, 0.0).astype(F32),
            jnp.zeros((2, 64), F32),
        ], axis=0) for i in (0, 1)], axis=1)
    for i in (0, 1):
        ids[g, i] = irow[i, 1:2]
    arrived(cores_other[0], cr_r.at[0])
    stage[...] = jnp.zeros_like(stage)
    stage[:, 0:H] = pboth[...]
    xp[...] = stage[...].T
    for s in range(PARTS):
        ga[s, g, 0:SIZES[s]] = xp[pl.ds(pl.multiple_of(own_row + offset(s, c), 16), SIZES[s])].astype(BF16)
        gather(ga, s, 0)

    for copy in local[len(small):]:
        copy.wait()
    load_all = ld[...].astype(BF16)
    for j in range(2):
        block = pt[pl.ds(pl.multiple_of(512 * c + 256 * j, 256), 256)]
        f0full[j] = lax.dot_general(load_all, block, NT, preferred_element_type=F32)
        f0[2 * c + j] = f0full[j, pl.ds(own_row, HALF)]
    own_pairs = pl.ds(2 * c, 2)
    push(f0full.at[:, pl.ds(other_row, HALF)], f0.at[own_pairs], ex_s.at[11], ex_r.at[11], sibling)

    stage[...] = jnp.zeros_like(stage)
    stage[0:25, 0:H] = ramp_v[...]
    stage[25:26, 0:H] = energy_v[...].reshape(1, H)
    ramp_t[...] = stage[...].T
    marginal, quad, cap, width = (pm[i:i + 1] for i in range(4))
    live = pm[5:6]
    for d in range(0, REACH + 1):
        keep = (width > d - 0.5).astype(F32)
        for o in ((0,) if d == 0 else (d, -d)):
            row = REACH + o
            column = ramp_t[own_ext, row:row + 1]
            if d == 0:
                kt[row] = jnp.broadcast_to(1.0 + column, (EXT, 128))
            else:
                kt[row] = column * keep
    bus_row = lax.broadcasted_iota(jnp.int32, (2048, 128), 0)
    oh[...] = jnp.where(bus_row == pm[4:5].astype(jnp.int32), 1.0, 0.0).astype(BF16)

    arrived(pt.at[other_block], ex_r.at[3])
    arrived(ids.at[pl.ds(0, 15)], id_r.at[0])

    def plant_columns(j, _):
        i = 4 * c + j
        bus = jnp.concatenate([ids[2 * i + a, b] for a in (0, 1) for b in (0, 1)], axis=1)
        iota = lax.broadcasted_iota(jnp.int32, (2048, 256), 0)
        one_hot = jnp.where(iota == bus, 1.0, 0.0).astype(BF16)
        q[i] = jnp.dot(pt[...], one_hot, preferred_element_type=F32).astype(BF16)
        push(q.at[i], q.at[i], q_s.at[j], q_r.at[j], sibling)
        return 0

    core_row = pl.multiple_of(48 * c, 16)
    halo_at = pl.multiple_of(HALF * other, 16)

    def ext_part(s):
        return pl.ds(pl.multiple_of(core_row + offset(s, c), 16), SIZES[s])

    def price_part(s):
        px[ext_part(s)] = jnp.dot(gathered(ga, s, 0), oh[...], preferred_element_type=F32)

    vb[...] = jnp.zeros_like(vb)
    vbe[...] = jnp.zeros_like(vbe)
    lax.fori_loop(0, 2, plant_columns, 0)
    price_part(0)
    halo_s[0] = px[ext_part(0)]
    push(halo_s.at[0], halo_p.at[0], ex_s.at[6], ex_r.at[6], sibling)
    arrived(cores_other[7], cr_r.at[7])
    stage[:, 0:H] = dboth[...]
    xd[...] = stage[...].T
    dsp[...] = xd[own_ext]
    def sweep(_, carry):
        d = dsp[...]
        vb[16:16 + EXT] = d + 0.5 * (px[...] - marginal - quad * d)
        for r in range(0, EXT, 64):
            total = kt[REACH, r:r + 64] * vb[16 + r:16 + r + 64]
            for s in range(1, REACH + 1):
                for o in (s, -s):
                    total = total + kt[REACH + o, r:r + 64] * vb[16 + o + r:16 + o + r + 64]
            dsp[r:r + 64] = live * jnp.clip(total, 0.0, cap)
        return carry

    early_row = pl.multiple_of(48 * other, 16)

    def early_part(k):
        rows = pl.ds(early_row, HALF)
        price = px[rows]
        dse[...] = dsp[rows]

        first, last = 0, HALF
        for low, high in ((24, 120), (32, 112), (48, 96)):
            d = dse[first:last]
            vbe[16 + first:16 + last] = d + 0.5 * (price[first:last] - marginal - quad * d)
            for r in range(low, high, 48 if high - low == 96 else (high - low) // 2):
                size = 48 if high - low == 96 else (high - low) // 2
                at = pl.ds(pl.multiple_of(early_row + r, 8), size)
                total = kt[REACH, at] * vbe[16 + r:16 + r + size]
                for s in range(1, REACH + 1):
                    for o in (s, -s):
                        total = total + kt[REACH + o, at] * vbe[16 + o + r:16 + o + r + size]
                dse[r:r + size] = live * jnp.clip(total, 0.0, cap)
            first, last = low, high

        gb[k, 0, g, 0:HALO] = dse[HALO:2 * HALO].astype(BF16)
        gather(gb.at[k], 0, 1 + k)

    def other_parts(k):
        for s in range(1, PARTS):
            gb[k, s, g, 0:SIZES[s]] = dsp[ext_part(s)].astype(BF16)
            gather(gb.at[k], s, 1 + k)

    def flow(k, s):
        spread = gathered(gb.at[k], s, 1 + k)
        n = SIZES[s]
        rows = pl.ds(offset(s, c), n)
        for pair in range(4):
            part = jnp.dot(spread, qt[pair], preferred_element_type=F32) - f0[pair, rows]
            for j in (0, 1):
                fb[k, s, 2 * pair + j, 0:n] = part[:, 128 * j:128 * j + 128].astype(BF16)
        for d in (4, 3, 5, 2, 6, 1, 7):
            target = (z + d) % 8
            push(fb.at[k, s, target, pl.ds(0, n)], rc.at[k, s, z, pl.ds(0, n)], zr_s.at[k, s],
                 zr_r.at[k, s], dev(target, g, c))

    def limit_lines(k, s):
        n = SIZES[s]
        arrived(rc.at[k, s, pl.ds(0, 7), pl.ds(0, n)], zr_r.at[k, s])
        total = fb[k, s, z, 0:n].astype(F32)
        for d in range(1, 8):
            total = total + rc[k, s, (z + d) % 8, 0:n].astype(F32)
        rows = pl.ds(offset(s, c), n)
        shifted = lps[rows] + total
        limit = lim[rows]
        new = shifted - jnp.clip(shifted, -limit, limit)
        lps[rows] = new
        sa[k, s, z, 0:n] = new.astype(BF16)
        block = sa.at[k, s, z, pl.ds(0, n)]
        for d in (4, 3, 5, 2, 6, 1, 7):
            push(block, block, zg_s.at[k, s], zg_r.at[k, s], dev((z + d) % 8, g, c))

    def congestion(k, s):
        n = SIZES[s]
        arrived(sa.at[k, s, pl.ds(0, 7), pl.ds(0, n)], zg_r.at[k, s])
        spread = jnp.concatenate([sa[k, s, i, 0:n] for i in range(8)], axis=1)
        for i in range(8):
            matrix = q[i] if k == 0 else pt[:, 256 * i:256 * i + 256]
            part = jnp.dot(spread, matrix, preferred_element_type=F32).astype(BF16)
            pb[k, s, 2 * i, 0:n] = part[:, 0:128]
            pb[k, s, 2 * i + 1, 0:n] = part[:, 128:256]
        for dx, dy in others:
            to = chip(dx, dy)
            push(pb.at[k, s, to, pl.ds(0, n)], rp.at[k, s, g, pl.ds(0, n)], rs_s.at[k, s], rs_r.at[k, s],
                 dev(z, to, c))

    def prices(k, s):
        n = SIZES[s]
        arrived(rp.at[k, s, pl.ds(0, 15), pl.ds(0, n)], rs_r.at[k, s])
        total = pb[k, s, g, 0:n].astype(F32)
        for d in range(1, 16):
            total = total + rp[k, s, (g + d) % 16, 0:n].astype(F32)
        row = pl.multiple_of(own_row + offset(s, c), 16)
        return ramp_t[pl.ds(row, n), 25:26] - total

    def drain(steps, refs):
        for ref, i in refs:
            sent_off(ref, ex_s.at[i])
        for s in range(PARTS):
            rows = pl.ds(0, SIZES[s])
            for k in (0, 1) if 0 in steps else (2,):
                sent_off(ga.at[s, pl.ds(0, 15), rows], ag_s.at[k, s])
            for k in steps:
                sent_off(rc.at[k, s, pl.ds(0, 7), rows], zr_s.at[k, s])
                sent_off(sa.at[k, s, pl.ds(0, 7), rows], zg_s.at[k, s])
                sent_off(rp.at[k, s, pl.ds(0, 15), rows], rs_s.at[k, s])
            if 1 in steps:
                sent_off(fin_s.at[rows], fin_ss.at[s])
                sent_off(lr.at[s, :, rows], lr_s.at[s])

    lax.fori_loop(2, 3 + no, plant_columns, 0)
    price_part(1)
    arrived(halo_p.at[0], ex_r.at[6])
    px[pl.ds(halo_at, HALO)] = halo_p[0]
    early_part(0)
    for s in range(2, PARTS):
        price_part(s)
    lax.fori_loop(0, ITERS, sweep, 0)
    other_parts(0)
    halo_s[1] = dsp[ext_part(0)]
    push(halo_s.at[1], halo_d, ex_s.at[7], ex_r.at[7], sibling)
    lax.fori_loop(3, 4 + no, plant_columns, 0)
    arrived(slim, ex_r.at[4])
    arrived(slps, ex_r.at[5])
    holds = c == z // 4
    lim[...] = jnp.where(holds, lim[...], slim[...])
    lps[...] = jnp.where(holds, lps[...], slps[...])
    arrived(f0.at[pl.ds(2 * other, 2)], ex_r.at[11])

    def transpose_columns(j, core):
        i = 4 * core + j
        for pair in range(4):
            qt[pair, pl.ds(pl.multiple_of(256 * i, 256), 256)] = q[i, 256 * pair:256 * pair + 256].T
        return core

    lax.fori_loop(0, 4, transpose_columns, c)
    for j in range(4):
        arrived(q.at[4 * other + j], q_r.at[j])
    lax.fori_loop(0, 4, transpose_columns, other)
    for s in range(PARTS):
        flow(0, s)
    for s in range(PARTS):
        limit_lines(0, s)
    for s in range(PARTS):
        congestion(0, s)
    px[ext_part(0)] = prices(0, 0)
    halo_s[2] = px[ext_part(0)]
    push(halo_s.at[2], halo_p.at[1], ex_s.at[8], ex_r.at[8], sibling)
    arrived(halo_d, ex_r.at[7])
    dsp[pl.ds(halo_at, HALO)] = halo_d[...]
    px[ext_part(1)] = prices(0, 1)
    arrived(halo_p.at[1], ex_r.at[8])
    px[pl.ds(halo_at, HALO)] = halo_p[1]

    early_part(1)
    for s in range(2, PARTS):
        px[ext_part(s)] = prices(0, s)
    lax.fori_loop(0, ITERS, sweep, 0)
    other_parts(1)
    fd_s[...] = dsp[pl.ds(core_row, HALF)]
    push(fd_s, fd_r, ex_s.at[9], ex_r.at[9], sibling)

    def rows_out(mine, theirs):
        gap = jnp.zeros((96, 128), F32)
        first = jnp.where(c == 0, mine, theirs)
        second = jnp.where(c == 0, theirs, mine)
        return jnp.concatenate([first, second, gap], axis=0).T

    arrived(fd_r, ex_r.at[9])
    stage[...] = rows_out(fd_s[...], fd_r[...])
    both_out[0] = stage[own_lanes, 0:H]
    for i, (ref, _) in enumerate(cores):
        sent_off(ref, cr_s.at[i])
    sent_off(ids.at[pl.ds(0, 15)], id_s.at[0])
    for j in range(4):
        sent_off(q.at[j], q_s.at[j])
    drain((0,), ((ptdf_in, 3), (slim, 4), (slps, 5), (f0.at[own_pairs], 11), (halo_s.at[0], 6), (halo_s.at[1], 7),
                 (halo_s.at[2], 8)))
    for s in range(PARTS):
        flow(1, s)
    for s in range(PARTS):
        limit_lines(1, s)
    for s in range(PARTS):
        congestion(1, s)
    for s in range(PARTS):
        push(sa.at[1, s, pl.ds(4 * other, 4), pl.ds(0, SIZES[s])], lr.at[s, :, pl.ds(0, SIZES[s])], lr_s.at[s],
             lr_r.at[s], sibling)
    for s in range(PARTS):
        rows = pl.ds(pl.multiple_of(own_row + offset(s, c), 16), SIZES[s])
        for i in range(4):
            line_out[rows, 128 * i:128 * i + 128] = sa[1, s, 4 * c + i, 0:SIZES[s]].astype(F32)
    for s in range(PARTS):
        rows = pl.ds(offset(s, c), SIZES[s])
        fin_s[rows] = prices(1, s)
        push(fin_s.at[rows], fin_r.at[rows], fin_ss.at[s], fin_rs.at[s], sibling)
    for s in range(PARTS):
        arrived(lr.at[s, :, pl.ds(0, SIZES[s])], lr_r.at[s])
        rows = pl.ds(pl.multiple_of(other_row + offset(s, other), 16), SIZES[s])
        for i in range(4):
            line_out[rows, 128 * i:128 * i + 128] = lr[s, i, 0:SIZES[s]].astype(F32)
    for s in range(PARTS):
        arrived(fin_r.at[pl.ds(offset(s, other), SIZES[s])], fin_rs.at[s])
    stage[...] = rows_out(fin_s[...], fin_r[...])
    both_out[1] = stage[own_lanes, 0:H]

    drain((1,), ((fd_s, 9),))


def shards(
    dispatch_start, marginal_cost, quad_cost, capacity, band_widths, ramp_band, plant_bus, plant_counts,
    load, ptdf, line_limit, line_price_start, bus_price_start, energy_price,
):
    vmem = pl.BlockSpec(memory_space=pltpu.VMEM)
    hbm = pl.BlockSpec(memory_space=pltpu.HBM)
    sem = pltpu.SemaphoreType.DMA

    def in_hbm(array):
        return pltpu.with_memory_space_constraint(array, pltpu.HBM)

    def v(shape, kind=F32):
        return pltpu.VMEM(shape, kind)

    scratch = [
        v((128, H)), v((128, H)), v((2, 3, 64)), v((2, 2, 64), jnp.int32), v((2, 1, 1), jnp.int32), v((25, H)), v((H,)),
        v((128, 384)), v((384, 128)), v((384, 128)), v((8, 128)), v((16, 2, 1, 64), jnp.int32),
        v((384, 128)), v((25, EXT, 128)), v((EXT + 32, 128)), v((EXT, 128)), v((EXT, 128)),
        v((2048, 128), BF16),
        v((1024, 2048), BF16), v((8, 1024, 256), BF16), v((4, 2048, 256), BF16), v((H, 2048)),
        v((HALF, 128)), v((HALF, 128)), v((HALF, 128)), v((HALF, 128)),
        v((4, HALF, 256)), v((2, H, 256)),
        v((PARTS, 16, MOST, 128), BF16), v((2, PARTS, 16, MOST, 128), BF16),
        v((2, PARTS, 8, MOST, 128), BF16), v((2, PARTS, 8, MOST, 128), BF16),
        v((2, PARTS, 8, MOST, 128), BF16),
        v((2, PARTS, 16, MOST, 128), BF16), v((2, PARTS, 16, MOST, 128), BF16),
        v((HALF + 32, 128)), v((HALF, 128)),
        v((3, HALO, 128)), v((2, HALO, 128)), v((HALO, 128)),
        v((HALF, 128)), v((HALF, 128)), v((HALF, 128)), v((HALF, 128)),
        v((PARTS, 4, MOST, 128), BF16),
        sem((14,)), sem((12,)), sem((12,)), sem((PARTS,)), sem((PARTS,)), sem((PARTS,)), sem((PARTS,)), sem((8,)), sem((8,)), sem((1,)), sem((1,)), sem((4,)), sem((4,)),
        sem((3, PARTS)), sem((3, PARTS)), sem((2, PARTS)), sem((2, PARTS)), sem((2, PARTS)), sem((2, PARTS)),
        sem((2, PARTS)), sem((2, PARTS)),
    ]
    both, line_price = pl.pallas_call(
        body,
        out_shape=(
            jax.ShapeDtypeStruct((2, 64, H), F32),
            jax.ShapeDtypeStruct((H, 512), F32),
        ),
        in_specs=[hbm] * 14,
        out_specs=(vmem,) * 2,
        scratch_shapes=scratch,
        compiler_params=pltpu.CompilerParams(
            collective_id=0, has_side_effects=True, vmem_limit_bytes=40 * 2**20),
        name="dispatch_window",
    )(
        *map(in_hbm, (dispatch_start, bus_price_start, marginal_cost[None], quad_cost[None], capacity[None],
                      band_widths[None], plant_bus[None])),
        plant_counts[None],
        *map(in_hbm, (ramp_band, energy_price, load.T, ptdf, line_limit.T, line_price_start.T)),
    )
    return both[0], line_price.T, both[1]


def solution(mesh):
    placed = (
        P(("region", "plant"), None),
        P(("region", "plant")),
        P(("region", "plant")),
        P(("region", "plant")),
        P(("region", "plant")),
        P(),
        P(("region", "plant")),
        P(("region", "plant")),
        P("region", None),
        P("plant", "region"),
        P("plant", None),
        P("plant", None),
        P(("region", "plant"), None),
        P(),
    )
    return jax.shard_map(
        shards,
        mesh=mesh,
        in_specs=placed,
        out_specs=(P(("region", "plant"), None), P("plant", None), P(("region", "plant"), None)),
        check_vma=False,
    )
```

```python
import jax
import jax.numpy as jnp
from jax import lax
from jax.experimental import pallas as pl
from jax.experimental.pallas import tpu as pltpu
from jax.sharding import PartitionSpec as P

H = 288
HALF = 144
EXT = 192
SIZES = (48, 48, 48)
STARTS = (0, 48, 96)
PARTS = len(SIZES)
MOST = max(SIZES)
HALO = 48
REACH = 12
ITERS = 3
F32 = jnp.float32
BF16 = jnp.bfloat16
NN = (((1,), (0,)), ((), ()))
NT = (((1,), (1,)), ((), ()))
FAR_FIRST = (2, 1, 3)


def body(
    dispatch_in, bus_price_in, marginal_in, quad_in, cap_in, width_in, bus_in, count_in, ramp_in, energy_in,
    load_in, ptdf_in, limit_in, lp_in,
    both_out, line_out,
    dboth, pboth, prow, irow, crow, ramp_v, energy_v, stage, xd, xp, pm, ids, ramp_t, kt, vb, dsp, px, oh,
    pt, q, qt, ld, lim, lps, slim, slps, f0, f0full,
    ga, gb, fb, rc, sa, pb, rp,
    vbe, dse, halo_s, halo_p, halo_d, fin_s, fin_r, fd_s, fd_r, lr,
    loc, ex_s, ex_r, lr_s, lr_r, fin_ss, fin_rs, cr_s, cr_r, id_s, id_r, q_s, q_r, ag_s, ag_r, zr_s, zr_r, zg_s, zg_r, rs_s, rs_r,
):
    z = lax.axis_index("region")
    p = lax.axis_index("plant")
    g = p // 2
    x = g // 4
    y = g % 4
    c = p % 2
    other = 1 - c
    no = z // 8

    def dev(zz, gg, cc):
        return (zz, gg * 2 + cc)

    sibling = dev(z, g, other)

    def chip(dx, dy):
        return ((x + dx) % 4) * 4 + (y + dy) % 4

    others = [(dx, dy) for dy in (2, 1, 3, 0) for dx in (2, 1, 3, 0) if dx or dy]

    def remote(src, dst, send, recv, device):
        return pltpu.make_async_remote_copy(
            src_ref=src, dst_ref=dst, send_sem=send, recv_sem=recv,
            device_id=device, device_id_type=pl.DeviceIdType.MESH,
        )

    def push(src, dst, send, recv, device):
        remote(src, dst, send, recv, device).start()

    def arrived(dst, recv):
        remote(dst, dst, ex_s.at[0], recv, sibling).wait_recv()

    def sent_off(src, send):
        remote(src, src, send, ex_r.at[0], sibling).wait_send()

    def offset(s, core):
        return pl.multiple_of(core * STARTS[s] + (1 - core) * (HALF - STARTS[s] - SIZES[s]), 16)

    barrier = pltpu.get_barrier_semaphore()
    peers = [sibling]
    peers += [dev(z, chip(*d), core) for d in others for core in (c, other)]
    peers += [dev((z + d) % 8, g, c) for d in range(1, 8)]
    for peer in peers:
        pl.semaphore_signal(barrier, inc=1, device_id=peer, device_id_type=pl.DeviceIdType.MESH)

    own_row = pl.multiple_of(HALF * c, 16)
    other_row = pl.multiple_of(HALF * other, 16)
    line_lane = pl.multiple_of(128 * (z % 4), 128)
    own_block = pl.ds(pl.multiple_of(512 * c, 512), 512)
    other_block = pl.ds(pl.multiple_of(512 * other, 512), 512)
    own_lanes = pl.ds(pl.multiple_of(64 * c, 64), 64)
    rows_in = [(marginal_in, 0), (quad_in, 1), (cap_in, 2)]
    cores = [
        (bus_price_in, pboth.at[own_lanes]),
        *[(ref, prow.at[c, i:i + 1]) for ref, i in rows_in],
        (width_in, irow.at[c, 0:1]), (bus_in, irow.at[c, 1:2]), (count_in, crow.at[c]),
        (dispatch_in, dboth.at[own_lanes]),
    ]
    other_lanes = pl.ds(pl.multiple_of(64 * other, 64), 64)
    cores_other = [pboth.at[other_lanes], *[prow.at[other, i:i + 1] for i in range(3)],
                   irow.at[other, 0:1], irow.at[other, 1:2], crow.at[other], dboth.at[other_lanes]]
    small = cores + [(ramp_in, ramp_v), (energy_in, energy_v)]
    large = [
        (load_in, ld),
        (ptdf_in, pt.at[own_block]),
        (limit_in.at[pl.ds(own_row, HALF), pl.ds(line_lane, 128)], lim),
        (lp_in.at[pl.ds(own_row, HALF), pl.ds(line_lane, 128)], lps),
    ]
    local = [pltpu.make_async_copy(src, dst, loc.at[i]) for i, (src, dst) in enumerate(small + large)]
    for copy in local:
        copy.start()

    own_ext = pl.ds(pl.multiple_of(96 * c, 96), EXT)
    stage[...] = jnp.zeros_like(stage)
    vb[...] = jnp.zeros_like(vb)
    vbe[...] = jnp.zeros_like(vbe)
    pl.semaphore_wait(barrier, len(peers))
    for i, (src, dst) in enumerate(cores):
        push(src, dst, cr_s.at[i], cr_r.at[i], sibling)
    for d in others:
        for core in (c, other):
            push(bus_in, ids.at[g, c], id_s.at[0], id_r.at[0], dev(z, chip(*d), core))
    push(ptdf_in, pt.at[own_block], ex_s.at[2], ex_r.at[2], sibling)
    push(limit_in.at[pl.ds(other_row, HALF), pl.ds(line_lane, 128)], slim, ex_s.at[3], ex_r.at[3], sibling)
    push(lp_in.at[pl.ds(other_row, HALF), pl.ds(line_lane, 128)], slps, ex_s.at[4], ex_r.at[4], sibling)

    def gather(grid, s, k):
        for d in others:
            block = grid.at[s, g, pl.ds(0, SIZES[s])]
            push(block, block, ag_s.at[k], ag_r.at[k, s], dev(z, chip(*d), c))

    def gathered(grid, s, k):
        arrived(grid.at[s, pl.ds(0, 15), pl.ds(0, SIZES[s])], ag_r.at[k, s])
        return jnp.concatenate([grid[s, i, 0:SIZES[s]] for i in range(16)], axis=1)

    local[0].wait()
    arrived(cores_other[0], cr_r.at[0])
    stage[:, 0:H] = pboth[...]
    xp[...] = stage[...].T
    for s in range(PARTS):
        ga[s, g, 0:SIZES[s]] = xp[pl.ds(pl.multiple_of(own_row + offset(s, c), 16), SIZES[s])].astype(BF16)
        gather(ga, s, 0)
    for copy in local[1:len(small)]:
        copy.wait()
    for i in range(1, 7):
        arrived(cores_other[i], cr_r.at[i])
    slot = lax.broadcasted_iota(jnp.int32, (1, 64), 1)
    pm[...] = jnp.concatenate([
        jnp.concatenate([
            prow[i], irow[i].astype(F32), jnp.where(slot < crow[i], 1.0, 0.0).astype(F32),
            jnp.zeros((2, 64), F32),
        ], axis=0) for i in (0, 1)], axis=1)
    for i in (0, 1):
        ids[g, i] = irow[i, 1:2]
    for copy in local[len(small):]:
        copy.wait()
    load_all = ld[...].astype(BF16)
    for j in range(2):
        block = pt[pl.ds(pl.multiple_of(512 * c + 256 * j, 256), 256)]
        f0full[j] = lax.dot_general(load_all, block, NT, preferred_element_type=F32)
        f0[2 * c + j] = f0full[j, pl.ds(own_row, HALF)]
    own_pairs = pl.ds(2 * c, 2)
    push(f0full.at[:, pl.ds(other_row, HALF)], f0.at[own_pairs], ex_s.at[0], ex_r.at[0], sibling)

    stage[...] = jnp.zeros_like(stage)
    stage[0:25, 0:H] = ramp_v[...]
    stage[25:26, 0:H] = energy_v[...].reshape(1, H)
    ramp_t[...] = stage[...].T
    marginal, quad, cap, width = (pm[i:i + 1] for i in range(4))
    live = pm[5:6]
    for d in range(0, REACH + 1):
        keep = (width > d - 0.5).astype(F32)
        for o in ((0,) if d == 0 else (d, -d)):
            row = REACH + o
            column = ramp_t[own_ext, row:row + 1]
            if d == 0:
                kt[row] = jnp.broadcast_to(1.0 + column, (EXT, 128))
            else:
                kt[row] = column * keep
    bus_row = lax.broadcasted_iota(jnp.int32, (2048, 128), 0)
    oh[...] = jnp.where(bus_row == pm[4:5].astype(jnp.int32), 1.0, 0.0).astype(BF16)

    arrived(pt.at[other_block], ex_r.at[2])
    arrived(ids.at[pl.ds(0, 15)], id_r.at[0])

    def plant_columns(j, _):
        i = 4 * c + j
        bus = jnp.concatenate([ids[2 * i + a, b] for a in (0, 1) for b in (0, 1)], axis=1)
        iota = lax.broadcasted_iota(jnp.int32, (2048, 256), 0)
        one_hot = jnp.where(iota == bus, 1.0, 0.0).astype(BF16)
        q[i] = jnp.dot(pt[...], one_hot, preferred_element_type=F32).astype(BF16)
        push(q.at[i], q.at[i], q_s.at[0], q_r.at[j], sibling)
        return 0

    core_row = pl.multiple_of(48 * c, 16)
    halo_at = pl.multiple_of(HALF * other, 16)

    def ext_part(s):
        return pl.ds(pl.multiple_of(core_row + offset(s, c), 16), SIZES[s])

    def price_part(s):
        px[ext_part(s)] = jnp.dot(gathered(ga, s, 0), oh[...], preferred_element_type=F32)

    lax.fori_loop(0, 2, plant_columns, 0)
    price_part(0)
    halo_s[0] = px[ext_part(0)]
    push(halo_s.at[0], halo_p.at[0], ex_s.at[5], ex_r.at[5], sibling)
    arrived(cores_other[7], cr_r.at[7])
    stage[:, 0:H] = dboth[...]
    xd[...] = stage[...].T
    dsp[...] = xd[own_ext]
    def sweep(_, carry):
        d = dsp[...]
        vb[16:16 + EXT] = d + 0.5 * (px[...] - marginal - quad * d)
        for r in range(0, EXT, 64):
            total = kt[REACH, r:r + 64] * vb[16 + r:16 + r + 64]
            for s in range(1, REACH + 1):
                for o in (s, -s):
                    total = total + kt[REACH + o, r:r + 64] * vb[16 + o + r:16 + o + r + 64]
            dsp[r:r + 64] = live * jnp.clip(total, 0.0, cap)
        return carry

    early_row = pl.multiple_of(48 * other, 16)

    def early_part(k):
        rows = pl.ds(early_row, HALF)
        price = px[rows]
        dse[...] = dsp[rows]

        first, last = 0, HALF
        for low, high in ((24, 120), (32, 112), (48, 96)):
            d = dse[first:last]
            vbe[16 + first:16 + last] = d + 0.5 * (price[first:last] - marginal - quad * d)
            for r in range(low, high, 48 if high - low == 96 else (high - low) // 2):
                size = 48 if high - low == 96 else (high - low) // 2
                at = pl.ds(pl.multiple_of(early_row + r, 8), size)
                total = kt[REACH, at] * vbe[16 + r:16 + r + size]
                for s in range(1, REACH + 1):
                    for o in (s, -s):
                        total = total + kt[REACH + o, at] * vbe[16 + o + r:16 + o + r + size]
                dse[r:r + size] = live * jnp.clip(total, 0.0, cap)
            first, last = low, high

        gb[k, 0, g, 0:HALO] = dse[HALO:2 * HALO].astype(BF16)
        gather(gb.at[k], 0, 1 + k)

    def other_parts(k):
        for s in range(1, PARTS):
            gb[k, s, g, 0:SIZES[s]] = dsp[ext_part(s)].astype(BF16)
            gather(gb.at[k], s, 1 + k)

    def flow(k, s):
        spread = gathered(gb.at[k], s, 1 + k)
        n = SIZES[s]
        rows = pl.ds(offset(s, c), n)
        for pair in range(4):
            part = jnp.dot(spread, qt[pair], preferred_element_type=F32) - f0[pair, rows]
            for j in (0, 1):
                fb[k, s, 2 * pair + j, 0:n] = part[:, 128 * j:128 * j + 128].astype(BF16)
        for d in (4, 3, 5, 2, 6, 1, 7):
            target = (z + d) % 8
            push(fb.at[k, s, target, pl.ds(0, n)], rc.at[k, s, z, pl.ds(0, n)], zr_s.at[k],
                 zr_r.at[k, s], dev(target, g, c))

    def limit_lines(k, s):
        n = SIZES[s]
        arrived(rc.at[k, s, pl.ds(0, 7), pl.ds(0, n)], zr_r.at[k, s])
        total = fb[k, s, z, 0:n].astype(F32)
        for d in range(1, 8):
            total = total + rc[k, s, (z + d) % 8, 0:n].astype(F32)
        rows = pl.ds(offset(s, c), n)
        shifted = lps[rows] + total
        limit = lim[rows]
        new = shifted - jnp.clip(shifted, -limit, limit)
        lps[rows] = new
        sa[k, s, z, 0:n] = new.astype(BF16)
        block = sa.at[k, s, z, pl.ds(0, n)]
        for d in (4, 3, 5, 2, 6, 1, 7):
            push(block, block, zg_s.at[k], zg_r.at[k, s], dev((z + d) % 8, g, c))

    def congestion(k, s):
        n = SIZES[s]
        arrived(sa.at[k, s, pl.ds(0, 7), pl.ds(0, n)], zg_r.at[k, s])
        spread = jnp.concatenate([sa[k, s, i, 0:n] for i in range(8)], axis=1)
        for i in range(8):
            matrix = q[i] if k == 0 else pt[:, 256 * i:256 * i + 256]
            part = jnp.dot(spread, matrix, preferred_element_type=F32).astype(BF16)
            pb[k, s, 2 * i, 0:n] = part[:, 0:128]
            pb[k, s, 2 * i + 1, 0:n] = part[:, 128:256]
        for dx, dy in others:
            to = chip(dx, dy)
            push(pb.at[k, s, to, pl.ds(0, n)], rp.at[k, s, g, pl.ds(0, n)], rs_s.at[k], rs_r.at[k, s],
                 dev(z, to, c))

    def prices(k, s):
        n = SIZES[s]
        arrived(rp.at[k, s, pl.ds(0, 15), pl.ds(0, n)], rs_r.at[k, s])
        total = pb[k, s, g, 0:n].astype(F32)
        for d in range(1, 16):
            total = total + rp[k, s, (g + d) % 16, 0:n].astype(F32)
        row = pl.multiple_of(own_row + offset(s, c), 16)
        return ramp_t[pl.ds(row, n), 25:26] - total

    def drain(steps, refs):
        for ref, i in refs:
            sent_off(ref, ex_s.at[i])
        for k in (0, 1) if 0 in steps else (2,):
            sent_off(ga.at[:, pl.ds(0, 15)], ag_s.at[k])
        for k in steps:
            sent_off(rc.at[k, :, pl.ds(0, 7)], zr_s.at[k])
            sent_off(sa.at[k, :, pl.ds(0, 7)], zg_s.at[k])
            sent_off(rp.at[k, :, pl.ds(0, 15)], rs_s.at[k])
        if 1 in steps:
            sent_off(fin_s, fin_ss.at[0])
            sent_off(lr, lr_s.at[0])

    lax.fori_loop(2, 3 + no, plant_columns, 0)
    price_part(1)
    arrived(halo_p.at[0], ex_r.at[5])
    px[pl.ds(halo_at, HALO)] = halo_p[0]
    early_part(0)
    for s in range(2, PARTS):
        price_part(s)
    lax.fori_loop(0, ITERS, sweep, 0)
    other_parts(0)
    halo_s[1] = dsp[ext_part(0)]
    push(halo_s.at[1], halo_d, ex_s.at[5], ex_r.at[6], sibling)
    lax.fori_loop(3, 4 + no, plant_columns, 0)
    arrived(slim, ex_r.at[3])
    arrived(slps, ex_r.at[4])
    holds = c == z // 4
    lim[...] = jnp.where(holds, lim[...], slim[...])
    lps[...] = jnp.where(holds, lps[...], slps[...])
    arrived(f0.at[pl.ds(2 * other, 2)], ex_r.at[0])

    def transpose_columns(j, core):
        i = 4 * core + j
        for pair in range(4):
            qt[pair, pl.ds(pl.multiple_of(256 * i, 256), 256)] = q[i, 256 * pair:256 * pair + 256].T
        return core

    lax.fori_loop(0, 4, transpose_columns, c)
    for j in range(4):
        arrived(q.at[4 * other + j], q_r.at[j])
    lax.fori_loop(0, 4, transpose_columns, other)
    for s in range(PARTS):
        flow(0, s)
    for s in range(PARTS):
        limit_lines(0, s)
    for s in range(PARTS):
        congestion(0, s)
    px[ext_part(0)] = prices(0, 0)
    halo_s[2] = px[ext_part(0)]
    push(halo_s.at[2], halo_p.at[1], ex_s.at[5], ex_r.at[7], sibling)
    arrived(halo_d, ex_r.at[6])
    dsp[pl.ds(halo_at, HALO)] = halo_d[...]
    px[ext_part(1)] = prices(0, 1)
    arrived(halo_p.at[1], ex_r.at[7])
    px[pl.ds(halo_at, HALO)] = halo_p[1]

    early_part(1)
    for s in range(2, PARTS):
        px[ext_part(s)] = prices(0, s)
    lax.fori_loop(0, ITERS, sweep, 0)
    other_parts(1)
    fd_s[...] = dsp[pl.ds(core_row, HALF)]
    push(fd_s, fd_r, ex_s.at[1], ex_r.at[1], sibling)

    def rows_out(mine, theirs):
        gap = jnp.zeros((96, 128), F32)
        first = jnp.where(c == 0, mine, theirs)
        second = jnp.where(c == 0, theirs, mine)
        return jnp.concatenate([first, second, gap], axis=0).T

    arrived(fd_r, ex_r.at[1])
    stage[...] = rows_out(fd_s[...], fd_r[...])
    both_out[0] = stage[own_lanes, 0:H]
    for i, (ref, _) in enumerate(cores):
        sent_off(ref, cr_s.at[i])
    sent_off(ids.at[pl.ds(0, 15)], id_s.at[0])
    sent_off(q.at[pl.ds(0, 4)], q_s.at[0])
    drain((0,), ((ptdf_in, 2), (slim, 3), (slps, 4), (f0.at[own_pairs], 0), (halo_s, 5)))
    for s in range(PARTS):
        flow(1, s)
    for s in range(PARTS):
        limit_lines(1, s)
    for s in range(PARTS):
        congestion(1, s)
    for s in range(PARTS):
        push(sa.at[1, s, pl.ds(4 * other, 4), pl.ds(0, SIZES[s])], lr.at[s, :, pl.ds(0, SIZES[s])], lr_s.at[0],
             lr_r.at[s], sibling)
    for s in range(PARTS):
        rows = pl.ds(pl.multiple_of(own_row + offset(s, c), 16), SIZES[s])
        for i in range(4):
            line_out[rows, 128 * i:128 * i + 128] = sa[1, s, 4 * c + i, 0:SIZES[s]].astype(F32)
    for s in range(PARTS):
        rows = pl.ds(offset(s, c), SIZES[s])
        fin_s[rows] = prices(1, s)
        push(fin_s.at[rows], fin_r.at[rows], fin_ss.at[0], fin_rs.at[s], sibling)
    for s in range(PARTS):
        arrived(lr.at[s, :, pl.ds(0, SIZES[s])], lr_r.at[s])
        rows = pl.ds(pl.multiple_of(other_row + offset(s, other), 16), SIZES[s])
        for i in range(4):
            line_out[rows, 128 * i:128 * i + 128] = lr[s, i, 0:SIZES[s]].astype(F32)
    for s in range(PARTS):
        arrived(fin_r.at[pl.ds(offset(s, other), SIZES[s])], fin_rs.at[s])
    stage[...] = rows_out(fin_s[...], fin_r[...])
    both_out[1] = stage[own_lanes, 0:H]

    drain((1,), ((fd_s, 1),))


def shards(
    dispatch_start, marginal_cost, quad_cost, capacity, band_widths, ramp_band, plant_bus, plant_counts,
    load, ptdf, line_limit, line_price_start, bus_price_start, energy_price,
):
    vmem = pl.BlockSpec(memory_space=pltpu.VMEM)
    hbm = pl.BlockSpec(memory_space=pltpu.HBM)
    sem = pltpu.SemaphoreType.DMA

    def in_hbm(array):
        return pltpu.with_memory_space_constraint(array, pltpu.HBM)

    def v(shape, kind=F32):
        return pltpu.VMEM(shape, kind)

    scratch = [
        v((128, H)), v((128, H)), v((2, 3, 64)), v((2, 2, 64), jnp.int32), v((2, 1, 1), jnp.int32), v((25, H)), v((H,)),
        v((128, 384)), v((384, 128)), v((384, 128)), v((8, 128)), v((16, 2, 1, 64), jnp.int32),
        v((384, 128)), v((25, EXT, 128)), v((EXT + 32, 128)), v((EXT, 128)), v((EXT, 128)),
        v((2048, 128), BF16),
        v((1024, 2048), BF16), v((8, 1024, 256), BF16), v((4, 2048, 256), BF16), v((H, 2048)),
        v((HALF, 128)), v((HALF, 128)), v((HALF, 128)), v((HALF, 128)),
        v((4, HALF, 256)), v((2, H, 256)),
        v((PARTS, 16, MOST, 128), BF16), v((2, PARTS, 16, MOST, 128), BF16),
        v((2, PARTS, 8, MOST, 128), BF16), v((2, PARTS, 8, MOST, 128), BF16),
        v((2, PARTS, 8, MOST, 128), BF16),
        v((2, PARTS, 16, MOST, 128), BF16), v((2, PARTS, 16, MOST, 128), BF16),
        v((HALF + 32, 128)), v((HALF, 128)),
        v((3, HALO, 128)), v((2, HALO, 128)), v((HALO, 128)),
        v((HALF, 128)), v((HALF, 128)), v((HALF, 128)), v((HALF, 128)),
        v((PARTS, 4, MOST, 128), BF16),
        sem((14,)), sem((8,)), sem((8,)), sem((1,)), sem((PARTS,)), sem((1,)), sem((PARTS,)), sem((8,)), sem((8,)), sem((1,)), sem((1,)), sem((1,)), sem((4,)),
        sem((3,)), sem((3, PARTS)), sem((2,)), sem((2, PARTS)), sem((2,)), sem((2, PARTS)),
        sem((2,)), sem((2, PARTS)),
    ]
    both, line_price = pl.pallas_call(
        body,
        out_shape=(
            jax.ShapeDtypeStruct((2, 64, H), F32),
            jax.ShapeDtypeStruct((H, 512), F32),
        ),
        in_specs=[hbm] * 14,
        out_specs=(vmem,) * 2,
        scratch_shapes=scratch,
        compiler_params=pltpu.CompilerParams(
            collective_id=0, has_side_effects=True, vmem_limit_bytes=40 * 2**20),
        name="dispatch_window",
    )(
        *map(in_hbm, (dispatch_start, bus_price_start, marginal_cost[None], quad_cost[None], capacity[None],
                      band_widths[None], plant_bus[None])),
        plant_counts[None],
        *map(in_hbm, (ramp_band, energy_price, load.T, ptdf, line_limit.T, line_price_start.T)),
    )
    return both[0], line_price.T, both[1]


def solution(mesh):
    placed = (
        P(("region", "plant"), None),
        P(("region", "plant")),
        P(("region", "plant")),
        P(("region", "plant")),
        P(("region", "plant")),
        P(),
        P(("region", "plant")),
        P(("region", "plant")),
        P("region", None),
        P("plant", "region"),
        P("plant", None),
        P("plant", None),
        P(("region", "plant"), None),
        P(),
    )
    return jax.shard_map(
        shards,
        mesh=mesh,
        in_specs=placed,
        out_specs=(P(("region", "plant"), None), P("plant", None), P(("region", "plant"), None)),
        check_vma=False,
    )
```
